256 devices in a mesh: pair: 2 (over x_hi), row: 8 (over z), col: 16 (over y, x_lo, core).
Axes of the slice: x: 4 (x_hi: 2, x_lo: 2; x = x_hi * 2 + x_lo), y: 4, z: 8, core: 2. Of those that a mesh axis runs over, the one named last changes fastest.
Arguments:
- front_init: float32 [12288, 12288], P('row', ('pair', 'col')), may hold values from -24 to 24, as said below
- child_blocks: float32 [2, 8192, 8192], P('pair', 'row', 'col'), may hold values from -24 to 24, as said below
- tile_map: int32 [2, 64], replicated, may hold values from 0 to 95, as said below
Outputs:
- front_out: float32 [12288, 12288], P('row', ('pair', 'col'))
The draws below stay inside these ranges and needn't reach their ends.
Inputs may be any that keep to these rules, and one draw needn't show every extreme that they name: `front_init`: symmetric positive definite in natural order, with smallest eigenvalue 0.5 or more. `child_blocks`: each sibling's block is symmetric positive definite in natural order. tile_map[s, i] mod (32) equals i mod (32); within each such residue class each sibling's map is increasing, and every parent tile is named by at least one of the two siblings.
All inputs are finite; a program needn't handle non-finite values.
Results may differ from the reference program's by a relative error of at most 0.0001.
Values sent between devices are 32-bit elements; how exact they have to be, the bound alone decides.
No kernel may reach another device: no remote copies, remote signals or barrier semaphores. Data moves between devices by JAX's collectives and lax.ppermute only.
A program may use at most 64 MiB of HBM per device.

```python
import jax
import jax.numpy as jnp
from jax import lax

F = 12288
C = 8192
NPIV = 1024
TILE = 128
PANEL = 512
N_PAIR = 2
N_ROW = 8
N_COL = 16


def stored_order_drawn(matrix, parts, axis):
    moved = jnp.moveaxis(matrix, axis, 0)
    tiles = moved.shape[0] // TILE
    shaped = moved.reshape((tiles // parts, parts, TILE) + moved.shape[1:])
    shaped = jnp.swapaxes(shaped, 0, 1).reshape(moved.shape)
    return jnp.moveaxis(shaped, 0, axis)


def gram_plus(factor):
    gram = jnp.dot(factor, factor.T, precision=lax.Precision.HIGHEST) / factor.shape[1]
    return gram + 0.5 * jnp.eye(factor.shape[0], dtype=jnp.float32)


def draw_front_init(key, part):
    key = jax.random.fold_in(key, 11)
    first_key = jax.random.fold_in(key, 0)
    factor = jax.random.uniform(first_key, (F, NPIV), jnp.float32, -1.7320508, 1.7320508)
    natural = gram_plus(factor)
    return stored_order_drawn(stored_order_drawn(natural, N_ROW, 0), N_PAIR * N_COL, 1)


def draw_child_blocks(key, part):
    key = jax.random.fold_in(key, 23)
    blocks = []
    for sibling in range(2):
        first_key = jax.random.fold_in(jax.random.fold_in(key, sibling), 0)
        factor = jax.random.uniform(first_key, (C, NPIV), jnp.float32, -1.7320508, 1.7320508)
        natural = gram_plus(factor)
        blocks.append(stored_order_drawn(stored_order_drawn(natural, N_ROW, 0), N_COL, 1))
    return jnp.stack(blocks)


def draw_tile_map(key, part):
    key = jax.random.fold_in(key, 37)
    classes = N_PAIR * N_COL
    slots = F // TILE // classes
    chosen = C // TILE // classes
    missing = slots - chosen
    orders = jax.vmap(lambda one_key: jax.random.permutation(one_key, slots))(jax.random.split(key, classes))
    positions = jnp.arange(slots, dtype=jnp.int32)
    maps = []
    for sibling in range(2):
        dropped = orders[:, sibling * missing:(sibling + 1) * missing]
        flagged = jnp.any(dropped[:, :, None] == positions[None, None, :], axis=1).astype(jnp.int32)
        ranked = jnp.argsort(flagged * slots + positions[None, :], axis=1)[:, :chosen]
        parents = jnp.arange(classes, dtype=jnp.int32)[:, None] + classes * ranked
        maps.append(parents.T.reshape(-1))
    return jnp.stack(maps).astype(jnp.int32)


def setup_inputs(seed: int = 0) -> dict:
    arg_keys = jax.random.split(jax.random.key(seed), 4)
    return {
        "front_init": draw_front_init(jax.random.fold_in(arg_keys[3], 71), 0),
        "child_blocks": draw_child_blocks(jax.random.fold_in(arg_keys[3], 71), 0),
        "tile_map": draw_tile_map(jax.random.fold_in(arg_keys[3], 71), 0),
    }


def natural_order(matrix, parts, axis):
    moved = jnp.moveaxis(matrix, axis, 0)
    tiles = moved.shape[0] // TILE
    shaped = moved.reshape((parts, tiles // parts, TILE) + moved.shape[1:])
    shaped = jnp.swapaxes(shaped, 0, 1).reshape(moved.shape)
    return jnp.moveaxis(shaped, 0, axis)

def stored_order(matrix, parts, axis):
    moved = jnp.moveaxis(matrix, axis, 0)
    tiles = moved.shape[0] // TILE
    shaped = moved.reshape((tiles // parts, parts, TILE) + moved.shape[1:])
    shaped = jnp.swapaxes(shaped, 0, 1).reshape(moved.shape)
    return jnp.moveaxis(shaped, 0, axis)

def reference(front_init, child_blocks, tile_map):
    column_parts = N_PAIR * N_COL
    assembled = natural_order(natural_order(front_init, N_ROW, 0), column_parts, 1)
    parent_tiles = F // TILE
    child_tiles = C // TILE
    for sibling in range(2):
        contribution = natural_order(natural_order(child_blocks[sibling], N_ROW, 0), N_COL, 1)
        contribution = contribution.reshape(child_tiles, TILE, child_tiles, TILE).transpose(0, 2, 1, 3)
        tiled_front = assembled.reshape(parent_tiles, TILE, parent_tiles, TILE).transpose(0, 2, 1, 3)
        targets = tile_map[sibling].astype(jnp.int32)
        tiled_front = tiled_front.at[targets[:, None], targets[None, :]].add(contribution)
        assembled = tiled_front.transpose(0, 2, 1, 3).reshape(F, F)
    for offset in range(0, NPIV, PANEL):
        finish = offset + PANEL
        leading = jnp.linalg.cholesky(assembled[offset:finish, offset:finish])
        beneath = lax.linalg.triangular_solve(leading, assembled[finish:, offset:finish], left_side=False, lower=True, transpose_a=True)
        trailing = assembled[finish:, finish:] - jnp.dot(beneath, beneath.T, precision=lax.Precision.HIGHEST)
        square = jnp.tril(leading) + jnp.triu(leading.T, 1)
        assembled = assembled.at[offset:finish, offset:finish].set(square)
        assembled = assembled.at[finish:, offset:finish].set(beneath)
        assembled = assembled.at[offset:finish, finish:].set(beneath.T)
        assembled = assembled.at[finish:, finish:].set(trailing)
    return stored_order(stored_order(assembled, N_ROW, 0), column_parts, 1)
```

```python
import jax
import jax.numpy as jnp
from jax import lax
from jax.experimental import pallas as pl
from jax.experimental.pallas import tpu as pltpu
from jax.sharding import PartitionSpec as P

TILE = 128
PIVOT_TILES = 8
NPIV = TILE * PIVOT_TILES
STRIP = 32
EXACT = lax.Precision.HIGHEST


def exact_dot(a, b, contract=((1,), (0,))):
    return lax.dot_general(
        a, b, (contract, ((), ())), precision=EXACT, preferred_element_type=jnp.float32
    )


def split(x):
    high = x.astype(jnp.bfloat16)
    low = (x - high.astype(jnp.float32)).astype(jnp.bfloat16)
    return high, low


def split_dot(a, b, contract):
    dims = (contract, ((), ()))
    a_high, a_low = a
    b_high, b_low = b

    def one(x, y):
        return lax.dot_general(x, y, dims, preferred_element_type=jnp.float32)

    return one(a_high, b_high) + (one(a_high, b_low) + one(a_low, b_high))


def factor_tile(block):
    row = lax.broadcasted_iota(jnp.int32, (TILE, TILE), 0)
    lane = lax.broadcasted_iota(jnp.int32, (TILE, TILE), 1)
    remaining = jnp.concatenate([block, (row == lane).astype(jnp.float32)], axis=1)
    strip_row = lax.broadcasted_iota(jnp.int32, (STRIP, 1), 0)
    wide_row = lax.broadcasted_iota(jnp.int32, (STRIP, 2 * TILE), 0)
    wide_lane = lax.broadcasted_iota(jnp.int32, (STRIP, 2 * TILE), 1)
    done = []
    for first in range(0, TILE, STRIP):
        strip = remaining[:STRIP]
        for k in range(STRIP):
            at = first + k
            column = strip[:, at : at + 1]
            pivot_row = strip[k : k + 1]
            pivot = strip[k : k + 1, at : at + 1]
            factor = jnp.where(strip_row > k, column * (1.0 / pivot), 0.0)
            strip = strip - factor * pivot_row
        diagonal = jnp.sum(
            jnp.where(wide_lane == wide_row + first, strip, 0.0), axis=1, keepdims=True
        )
        root = lax.rsqrt(diagonal)
        root = root * (1.5 - 0.5 * diagonal * root * root)
        strip = strip * root
        done.append(strip)
        if first + STRIP < TILE:
            change = exact_dot(strip[:, :TILE], strip, ((0,), (0,)))
            remaining = remaining[STRIP:] - change[first + STRIP :]
    whole = jnp.concatenate(done, axis=0)
    return jnp.where(lane >= row, whole[:, :TILE], 0.0), whole[:, TILE:]


def factor_kernel(parts_ref, upper_ref, lower_ref, inverse_ref):
    for i in range(PIVOT_TILES):
        for c in range(i, PIVOT_TILES):
            for k in range(4):
                upper_ref[pl.ds(i * TILE + k * 32, 32), pl.ds(c * TILE, TILE)] = parts_ref[k, c, i]

    def step(j, carry):
        at = pl.ds(pl.multiple_of(j * TILE, TILE), TILE)
        upper, inverse = factor_tile(upper_ref[at, at])
        upper_ref[at, at] = upper
        lower_ref[at, at] = upper.T
        inverse_ref[j] = inverse
        for now in range(PIVOT_TILES - 1):

            @pl.when(j == now)
            def _():
                here = slice(now * TILE, (now + 1) * TILE)
                after = slice((now + 1) * TILE, NPIV)
                solved = exact_dot(inverse, upper_ref[here, after])
                upper_ref[here, after] = solved
                lower_ref[after, here] = solved.T
                for k in range(now + 1, PIVOT_TILES):
                    rows = slice(k * TILE, (k + 1) * TILE)
                    rest = slice(k * TILE, NPIV)
                    offset = (k - now - 1) * TILE
                    upper_ref[rows, rest] = upper_ref[rows, rest] - exact_dot(
                        solved[:, offset : offset + TILE], solved[:, offset:], ((0,), (0,))
                    )

        return carry

    lax.fori_loop(0, PIVOT_TILES, step, 0)


def factor(parts):
    return pl.pallas_call(
        factor_kernel,
        out_shape=(
            jax.ShapeDtypeStruct((NPIV, NPIV), jnp.float32),
            jax.ShapeDtypeStruct((NPIV, NPIV), jnp.float32),
            jax.ShapeDtypeStruct((PIVOT_TILES, TILE, TILE), jnp.float32),
        ),
        in_specs=[pl.BlockSpec(memory_space=pltpu.VMEM)],
        out_specs=tuple(pl.BlockSpec(memory_space=pltpu.VMEM) for _ in range(3)),
        compiler_params=pltpu.CompilerParams(vmem_limit_bytes=40 * 2**20),
        cost_estimate=pl.CostEstimate(
            flops=60 * 10**9, bytes_accessed=13 * 2**20, transcendentals=0
        ),
        name="factor_pivots",
    )(parts)


def finish_kernel(
    meta_ref,
    front_ref,
    child_ref,
    received_ref,
    across_ref,
    beneath_ref,
    upper_ref,
    lower_ref,
    inverse_ref,
    out_ref,
    solved_ref,
    column_high_ref,
    column_low_ref,
    column_ref,
):
    group = pl.program_id(0)
    sibling = meta_ref[0]
    row_index = meta_ref[1]
    column_index = meta_ref[2]

    def solve(source, target_ref):
        for j in range(PIVOT_TILES):
            rows = slice(j * TILE, (j + 1) * TILE)
            rest = source(rows)
            if j:
                rest = rest - exact_dot(lower_ref[rows, : j * TILE], target_ref[: j * TILE, :])
            target_ref[rows, :] = exact_dot(inverse_ref[j], rest)

    @pl.when(group == 0)
    def _():
        solve(lambda rows: across_ref[rows, :], column_ref)
        high, low = split(column_ref[...])
        column_high_ref[...] = high
        column_low_ref[...] = low

    solve(lambda rows: beneath_ref[0, rows, :], solved_ref)
    update = split_dot(
        split(solved_ref[...]), (column_high_ref[...], column_low_ref[...]), ((0,), (0,))
    )

    def row_slot(s, u):
        return meta_ref[4 + s * 8 + group * 2 + u]

    def column_slot(s, u):
        return meta_ref[20 + s * 2 + u]

    for m in range(3):
        for n in range(3):
            lanes = slice(n * TILE, (n + 1) * TILE)
            total = front_ref[m, 0, :, lanes]
            for u in range(2):
                for v in range(2):
                    if m - u in (0, 1) and n - v in (0, 1):
                        own = (row_slot(sibling, u) == m) & (column_slot(sibling, v) == n)
                        other = (row_slot(1 - sibling, u) == m) & (
                            column_slot(1 - sibling, v) == n
                        )
                        mine = child_ref[
                            u, 0, :, pl.ds(pl.multiple_of((2 * v + sibling) * TILE, TILE), TILE)
                        ]
                        theirs = received_ref[u, 0, :, v * TILE : (v + 1) * TILE]
                        total = total + jnp.where(own, mine, 0.0)
                        total = total + jnp.where(other, theirs, 0.0)
            out_ref[m, 0, :, lanes] = (
                total - update[m * TILE : (m + 1) * TILE, n * TILE : (n + 1) * TILE]
            )

    pivot_column = column_index < PIVOT_TILES

    @pl.when(pivot_column)
    def _():
        rows = pl.ds(pl.multiple_of(column_index * TILE, TILE), TILE)
        for m in range(3):
            out_ref[m, 0, :, :TILE] = solved_ref[rows, m * TILE : (m + 1) * TILE].T

    @pl.when(group == 0)
    def _():
        rows = pl.ds(pl.multiple_of(row_index * TILE, TILE), TILE)
        out_ref[0, 0, :, :] = column_ref[rows, :]

        @pl.when(pivot_column)
        def _():
            columns = pl.ds(pl.multiple_of(column_index * TILE, TILE), TILE)
            above = upper_ref[rows, columns]
            below = lower_ref[rows, columns]

            @pl.when(row_index < column_index)
            def _():
                out_ref[0, 0, :, :TILE] = above

            @pl.when(row_index > column_index)
            def _():
                out_ref[0, 0, :, :TILE] = below

            @pl.when(row_index == column_index)
            def _():
                row = lax.broadcasted_iota(jnp.int32, (TILE, TILE), 0)
                lane = lax.broadcasted_iota(jnp.int32, (TILE, TILE), 1)
                out_ref[0, 0, :, :TILE] = jnp.where(row > lane, below, above)


def finish(meta, front, child, received, across, beneath, upper, lower, inverse):
    width = front.shape[1]
    whole = pl.BlockSpec(memory_space=pltpu.VMEM)
    out = pl.pallas_call(
        finish_kernel,
        grid=(4,),
        out_shape=jax.ShapeDtypeStruct((3, 4, TILE, width), jnp.float32),
        in_specs=[
            pl.BlockSpec(memory_space=pltpu.SMEM),
            pl.BlockSpec((3, 1, TILE, width), lambda g: (0, g, 0, 0)),
            pl.BlockSpec((2, 1, TILE, 4 * TILE), lambda g: (0, g, 0, 0)),
            pl.BlockSpec((2, 1, TILE, 2 * TILE), lambda g: (0, g, 0, 0)),
            whole,
            pl.BlockSpec((1, NPIV, width), lambda g: (g, 0, 0)),
            whole,
            whole,
            whole,
        ],
        out_specs=pl.BlockSpec((3, 1, TILE, width), lambda g: (0, g, 0, 0)),
        scratch_shapes=[
            pltpu.VMEM((NPIV, width), jnp.float32),
            pltpu.VMEM((NPIV, width), jnp.bfloat16),
            pltpu.VMEM((NPIV, width), jnp.bfloat16),
            pltpu.VMEM((NPIV, width), jnp.float32),
        ],
        compiler_params=pltpu.CompilerParams(vmem_limit_bytes=48 * 2**20),
        cost_estimate=pl.CostEstimate(
            flops=25 * 10**9, bytes_accessed=30 * 2**20, transcendentals=0
        ),
        name="solve_and_update",
    )(
        meta,
        front.reshape(3, 4, TILE, width),
        child.reshape(2, 4, TILE, 4 * TILE),
        received.reshape(2, 4, TILE, 2 * TILE),
        across,
        beneath,
        upper,
        lower,
        inverse,
    )
    return out.reshape(front.shape)


ALL = ("pair", "row", "col")


def at(pair, row, col):
    return (pair * 8 + row) * 16 + col


def body(front_init, child_blocks, tile_map):
    sibling = lax.axis_index("pair")
    row_index = lax.axis_index("row")
    col_index = lax.axis_index("col")
    column_index = sibling * 16 + col_index
    own = child_blocks[0]
    tiled_map = tile_map.astype(jnp.int32).reshape(2, 2, 32)
    positions = tiled_map // 32
    row_positions = jnp.swapaxes(
        lax.dynamic_index_in_dim(positions.reshape(2, 2, 4, 8), row_index, 3, keepdims=False), 1, 2
    )
    column_positions = lax.dynamic_index_in_dim(positions, column_index, 2, keepdims=False)
    meta = jnp.concatenate(
        [
            jnp.stack([sibling, row_index, column_index, column_index]),
            row_positions.reshape(16),
            column_positions.reshape(4),
        ]
    ).astype(jnp.int32)

    with jax.named_scope("pivot_rows"):
        first = own[:TILE].reshape(TILE, 2, 2, TILE)
        even, odd = first[:, :, 0], first[:, :, 1]
        kept = jnp.where(sibling == 0, even, odd)
        handed = jnp.where(sibling == 0, odd, even)
        received_first = lax.ppermute(handed, "pair", [(0, 1), (1, 0)])
        pieces = []
        own_row = row_positions[sibling, 0, 0] == 0
        other_row = row_positions[1 - sibling, 0, 0] == 0
        for n in range(3):
            total = front_init[:TILE, n * TILE : (n + 1) * TILE]
            for v in range(2):
                if n - v in (0, 1):
                    hit = own_row & (column_positions[sibling, v] == n)
                    total = total + jnp.where(hit, kept[:, v], 0.0)
                    hit = other_row & (column_positions[1 - sibling, v] == n)
                    total = total + jnp.where(hit, received_first[:, v], 0.0)
            pieces.append(total)
        pivot_rows = jnp.concatenate(pieces, axis=1)

    with jax.named_scope("pivot_block"):
        tile = pieces[0].reshape(4, 32, TILE)
        mine = tile[0]
        for k in range(1, 4):
            pair, half = divmod(k, 2)
            route = [
                (at(0, i, c), at(pair, i, c + 8 * half)) for i in range(8) for c in range(8)
            ]
            came = lax.ppermute(tile[k], ALL, route)
            mine = jnp.where((sibling == pair) & (col_index // 8 == half), came, mine)
        stacked = lax.all_gather(mine, "row")
        parts = lax.all_gather(stacked, ("pair", "col"))
        parts = parts.reshape(4, 8, 8, 32, TILE)

    with jax.named_scope("panel"):
        pivot_rows, parts = lax.optimization_barrier((pivot_rows, parts))
        across = lax.all_gather(pivot_rows, "row").reshape(NPIV, -1)
        route = []
        for pair in range(2):
            for i in range(8):
                for c in range(16):
                    half, other = divmod(c, 8)
                    route.append((at(pair, i, c), at(pair, other, 8 * half + i)))
        turned = lax.ppermute(pivot_rows, ALL, route)
        beneath = lax.all_gather(turned, ("pair", "col")).reshape(4, NPIV, -1)

    with jax.named_scope("siblings"):
        rows = own.reshape(NPIV, 2, 2, TILE)
        handed = jnp.where(sibling == 0, rows[:, :, 1], rows[:, :, 0]).reshape(NPIV, 2 * TILE)
        handed, parts = lax.optimization_barrier((handed, parts))
        received = lax.ppermute(handed, "pair", [(0, 1), (1, 0)])

    with jax.named_scope("factor"):
        upper, lower, inverse = factor(parts)
    with jax.named_scope("finish"):
        return finish(
            meta, front_init, own, received, across, beneath, upper, lower, inverse
        )


def solution(mesh):
    return jax.shard_map(
        body,
        mesh=mesh,
        in_specs=(P("row", ("pair", "col")), P("pair", "row", "col"), P()),
        out_specs=P("row", ("pair", "col")),
        check_vma=False,
    )
```

```python
import jax
import jax.numpy as jnp
from jax import lax
from jax.experimental import pallas as pl
from jax.experimental.pallas import tpu as pltpu
from jax.sharding import PartitionSpec as P

TILE = 128
PIVOT_TILES = 8
NPIV = TILE * PIVOT_TILES
STRIP = 64
GROUP = 8
PARTS = 2
FACTOR_FLOPS = 50 * 10**9
EXACT = lax.Precision.HIGHEST


def exact_dot(a, b, contract=((1,), (0,))):
    return lax.dot_general(
        a, b, (contract, ((), ())), precision=EXACT, preferred_element_type=jnp.float32
    )


def split(x):
    parts = []
    for _ in range(PARTS):
        part = x.astype(jnp.bfloat16)
        x = x - part.astype(jnp.float32)
        parts.append(part)
    return parts


def parts_dot(a, b, contract):
    total = None
    for order in reversed(range(len(a))):
        for i in range(order + 1):
            term = lax.dot_general(
                a[i], b[order - i], (contract, ((), ())), preferred_element_type=jnp.float32
            )
            total = term if total is None else total + term
    return total


def factor_tile(block):
    row = lax.broadcasted_iota(jnp.int32, (TILE, TILE), 0)
    lane = lax.broadcasted_iota(jnp.int32, (TILE, TILE), 1)
    remaining = jnp.concatenate([block, (row == lane).astype(jnp.float32)], axis=1)
    strip_row = lax.broadcasted_iota(jnp.int32, (STRIP, TILE), 0)

    def twice(x):
        return jnp.concatenate([x, x], axis=1)

    def tall(x):
        return jnp.concatenate([x] * (STRIP // 8), axis=0)

    done = []
    for first in range(0, TILE, STRIP):
        strip = remaining[:STRIP]
        for k in range(0, STRIP, GROUP):
            at = first + k
            columns, rows, corner, inverse = [], [], {}, []
            for t in range(GROUP):
                columns.append(jnp.broadcast_to(strip[:, at + t : at + t + 1], (STRIP, TILE)))
                rows.append(jnp.broadcast_to(strip[k + t : k + t + 1], (8, 2 * TILE)))
                for r in range(t + 1):
                    corner[r, t] = jnp.broadcast_to(
                        strip[k + r : k + r + 1, at + t : at + t + 1], (8, TILE)
                    )
            for r in range(GROUP):
                inverse.append(1.0 / corner[r, r])
                for t in range(r + 1, GROUP):
                    scale = corner[r, t] * inverse[r]
                    for u in range(t, GROUP):
                        corner[t, u] = corner[t, u] - scale * corner[r, u]
                    columns[t] = columns[t] - tall(scale) * columns[r]
                    rows[t] = rows[t] - twice(scale) * rows[r]
            beneath = strip
            if k + GROUP < STRIP:
                for t in range(GROUP):
                    share = jnp.where(strip_row >= k + GROUP, columns[t] * tall(inverse[t]), 0.0)
                    beneath = beneath - twice(share) * tall(rows[t])
            for t in range(GROUP):
                root = lax.rsqrt(corner[t, t])
                root = root * (1.5 - 0.5 * corner[t, t] * root * root)
                beneath = jnp.where(
                    twice(strip_row) == k + t, tall(rows[t] * twice(root)), beneath
                )
            strip = beneath
        done.append(strip)
        if first + STRIP < TILE:
            change = exact_dot(strip[:, :TILE], strip, ((0,), (0,)))
            remaining = remaining[STRIP:] - change[first + STRIP :]
    whole = jnp.concatenate(done, axis=0)
    return jnp.where(lane >= row, whole[:, :TILE], 0.0), whole[:, TILE:]


def factor_kernel(row_ref, parts_ref, upper_ref, inverse_ref):
    for i in range(PIVOT_TILES):
        away = i ^ row_ref[0]
        place = (away & 1) * 4 + (away & 2) + (away >> 2)
        for c in range(i, PIVOT_TILES):
            for half in range(2):
                upper_ref[pl.ds(i * TILE + half * 64, 64), pl.ds(c * TILE, TILE)] = parts_ref[
                    half * 8 + c, place
                ]

    def step(j, carry):
        at = pl.ds(pl.multiple_of(j * TILE, TILE), TILE)
        upper, inverse = factor_tile(upper_ref[at, at])
        upper_ref[at, at] = upper
        inverse_ref[j] = inverse.T
        for now in range(PIVOT_TILES - 1):

            @pl.when(j == now)
            def _():
                here = slice(now * TILE, (now + 1) * TILE)
                after = slice((now + 1) * TILE, NPIV)
                solved = exact_dot(inverse, upper_ref[here, after])
                upper_ref[here, after] = solved
                for k in range(now + 1, PIVOT_TILES):
                    rows = slice(k * TILE, (k + 1) * TILE)
                    rest = slice(k * TILE, NPIV)
                    offset = (k - now - 1) * TILE
                    upper_ref[rows, rest] = upper_ref[rows, rest] - exact_dot(
                        solved[:, offset : offset + TILE], solved[:, offset:], ((0,), (0,))
                    )

        return carry

    lax.fori_loop(0, PIVOT_TILES, step, 0)


def factor(row_index, parts):
    return pl.pallas_call(
        factor_kernel,
        out_shape=(
            jax.ShapeDtypeStruct((NPIV, NPIV), jnp.float32),
            jax.ShapeDtypeStruct((PIVOT_TILES, TILE, TILE), jnp.float32),
        ),
        in_specs=[
            pl.BlockSpec(memory_space=pltpu.SMEM),
            pl.BlockSpec(memory_space=pltpu.VMEM),
        ],
        out_specs=tuple(pl.BlockSpec(memory_space=pltpu.VMEM) for _ in range(2)),
        compiler_params=pltpu.CompilerParams(vmem_limit_bytes=24 * 2**20),
        cost_estimate=pl.CostEstimate(
            flops=FACTOR_FLOPS, bytes_accessed=9 * 2**20, transcendentals=0
        ),
        name="factor_pivots",
    )(row_index.astype(jnp.int32).reshape(1), parts)


def finish_kernel(
    meta_ref,
    front_ref,
    child_ref,
    received_ref,
    across_refs,
    beneath_ref,
    upper_ref,
    inverse_ref,
    out_ref,
    upper_parts_ref,
    wide_parts_ref,
    across_ref,
    solved_ref,
    solved_parts_ref,
):
    half_step = pl.program_id(0)
    sibling = meta_ref[0]
    row_index = meta_ref[1]
    column_index = meta_ref[2]
    width = across_ref.shape[1]
    column_rows = slice(2 * width, 3 * width)

    def solve(count, source):
        for j in range(PIVOT_TILES // 2):
            columns = slice(2 * j * TILE, 2 * (j + 1) * TILE)
            rest = jnp.concatenate([source(2 * j), source(2 * j + 1)], axis=1)
            if j:
                before = slice(0, 2 * j * TILE)
                rest = rest - parts_dot(
                    [ref[:count, before] for ref in solved_parts_ref],
                    [ref[before, columns] for ref in upper_parts_ref],
                    ((1,), (0,)),
                )
            result = parts_dot(split(rest), [ref[j] for ref in wide_parts_ref], ((1,), (0,)))
            solved_ref[:count, columns] = result
            for ref, part in zip(solved_parts_ref, split(result)):
                ref[:count, columns] = part

    def panel(i):
        return [beneath_ref[i, 0], beneath_ref[8 + i, 0]]

    @pl.when(half_step == 0)
    def _():
        for j in range(PIVOT_TILES // 2):
            rows = slice(2 * j * TILE, 2 * (j + 1) * TILE)
            after = slice(2 * (j + 1) * TILE, NPIV)
            if j < PIVOT_TILES // 2 - 1:
                for ref, part in zip(upper_parts_ref, split(upper_ref[rows, after])):
                    ref[rows, after] = part
            low, high = inverse_ref[2 * j], inverse_ref[2 * j + 1]
            between = upper_ref[
                2 * j * TILE : (2 * j + 1) * TILE, (2 * j + 1) * TILE : 2 * (j + 1) * TILE
            ]
            corner = -exact_dot(low, exact_dot(between, high))
            for ref, l, h, c in zip(wide_parts_ref, split(low), split(high), split(corner)):
                ref[j, :TILE, :TILE] = l
                ref[j, TILE:, TILE:] = h
                ref[j, :TILE, TILE:] = c
                ref[j, TILE:, :TILE] = jnp.zeros((TILE, TILE), jnp.bfloat16)

        for behind, ref in zip(RING, across_refs):
            across_ref[lax.rem(row_index - behind + 8, 8)] = ref[...]
        solve(3 * width, lambda i: jnp.concatenate(panel(i) + [across_ref[i]]))

    @pl.when(half_step > 0)
    def _():
        solve(2 * width, lambda i: jnp.concatenate(panel(i)))

    update = parts_dot(
        [ref[: 2 * width] for ref in solved_parts_ref],
        [ref[column_rows] for ref in solved_parts_ref],
        ((1,), (1,)),
    )

    for half in range(2):
        group = 2 * half_step + half

        def row_slot(s, u):
            return meta_ref[4 + s * 8 + group * 2 + u]

        def column_slot(s, u):
            return meta_ref[20 + s * 2 + u]

        for m in range(3):
            for n in range(3):
                lanes = slice(n * TILE, (n + 1) * TILE)
                total = front_ref[m, half, :, lanes]
                for u in range(2):
                    for v in range(2):
                        if m - u in (0, 1) and n - v in (0, 1):
                            own = (row_slot(sibling, u) == m) & (column_slot(sibling, v) == n)
                            other = (row_slot(1 - sibling, u) == m) & (
                                column_slot(1 - sibling, v) == n
                            )
                            own_lanes = pl.ds(
                                pl.multiple_of((2 * v + sibling) * TILE, TILE), TILE
                            )
                            mine = child_ref[u, half, :, own_lanes]
                            theirs = received_ref[v, u, half]
                            total = total + jnp.where(own, mine, 0.0)
                            total = total + jnp.where(other, theirs, 0.0)
                top = half * width + m * TILE
                out_ref[m, half, :, lanes] = (
                    total - update[top : top + TILE, n * TILE : (n + 1) * TILE]
                )

    pivot_column = column_index < PIVOT_TILES
    own_column = pl.ds(pl.multiple_of(lax.rem(column_index, 8) * TILE, TILE), TILE)

    @pl.when(pivot_column)
    def _():
        for half in range(2):
            for m in range(3):
                top = half * width + m * TILE
                out_ref[m, half, :, :TILE] = solved_ref[top : top + TILE, own_column]

    @pl.when(half_step == 0)
    def _():
        own_row = pl.ds(pl.multiple_of(row_index * TILE, TILE), TILE)
        for n in range(3):
            lanes = slice(n * TILE, (n + 1) * TILE)
            top = 2 * width + n * TILE
            out_ref[0, 0, :, lanes] = solved_ref[top : top + TILE, own_row].T

        @pl.when(pivot_column)
        def _():
            @pl.when(row_index < column_index)
            def _():
                out_ref[0, 0, :, :TILE] = upper_ref[own_row, own_column]

            @pl.when(row_index > column_index)
            def _():
                out_ref[0, 0, :, :TILE] = upper_ref[own_column, own_row].T

            @pl.when(row_index == column_index)
            def _():
                row = lax.broadcasted_iota(jnp.int32, (TILE, TILE), 0)
                lane = lax.broadcasted_iota(jnp.int32, (TILE, TILE), 1)
                tile = upper_ref[own_row, own_column]
                out_ref[0, 0, :, :TILE] = jnp.where(row > lane, tile.T, tile)


def finish(meta, front, child, received, across, beneath, upper, inverse):
    width = front.shape[1]
    whole = pl.BlockSpec(memory_space=pltpu.VMEM)
    held = lambda *shape: [pltpu.VMEM(shape, jnp.bfloat16) for _ in range(PARTS)]
    out = pl.pallas_call(
        finish_kernel,
        grid=(2,),
        out_shape=jax.ShapeDtypeStruct((3, 4, TILE, width), jnp.float32),
        in_specs=[
            pl.BlockSpec(memory_space=pltpu.SMEM),
            pl.BlockSpec((3, 2, TILE, width), lambda g: (0, g, 0, 0)),
            pl.BlockSpec((2, 2, TILE, 4 * TILE), lambda g: (0, g, 0, 0)),
            pl.BlockSpec((2, 2, 2, TILE, TILE), lambda g: (0, 0, g, 0, 0)),
            [whole] * 8,
            pl.BlockSpec((16, 1, width, TILE), lambda g: (0, g, 0, 0)),
            whole,
            whole,
        ],
        out_specs=pl.BlockSpec((3, 2, TILE, width), lambda g: (0, g, 0, 0)),
        scratch_shapes=[
            held(NPIV, NPIV),
            held(PIVOT_TILES // 2, 2 * TILE, 2 * TILE),
            pltpu.VMEM((8, width, TILE), jnp.float32),
            pltpu.VMEM((3 * width, NPIV), jnp.float32),
            held(3 * width, NPIV),
        ],
        compiler_params=pltpu.CompilerParams(vmem_limit_bytes=50 * 2**20),
        cost_estimate=pl.CostEstimate(
            flops=15 * 10**9, bytes_accessed=24 * 2**20, transcendentals=0
        ),
        name="solve_and_update",
    )(
        meta,
        front.reshape(3, 4, TILE, width),
        child.reshape(2, 4, TILE, 4 * TILE),
        received.reshape(2, 2, 4, TILE, TILE),
        across,
        beneath,
        upper,
        inverse,
    )
    return out.reshape(front.shape)


ALL = ("pair", "row", "col")
SWAP = [(0, 1), (1, 0)]
RING = (0, 1, 7, 2, 6, 3, 5, 4)


def at(pair, row, col):
    return (pair * 8 + row) * 16 + col


def ring_gather(block):
    up = [(i, (i + 1) % 8) for i in range(8)]
    down = [(i, (i - 1) % 8) for i in range(8)]
    half = block.shape[0] // 2
    behind = ahead = block
    blocks = [block]
    for _ in range(3):
        behind = lax.ppermute(behind, "row", up)
        ahead = lax.ppermute(ahead, "row", down)
        blocks += [behind, ahead]
    last = [lax.ppermute(behind[:half], "row", up), lax.ppermute(ahead[half:], "row", down)]
    return blocks + [jnp.concatenate(last)]


def assemble_kernel(meta_ref, front_ref, child_ref, came_ref, out_ref):
    sibling = meta_ref[0]
    own_row = meta_ref[4 + sibling * 8] == 0
    other_row = meta_ref[4 + (1 - sibling) * 8] == 0
    for n in range(3):
        total = front_ref[:, n * TILE : (n + 1) * TILE]
        for v in range(2):
            if n - v in (0, 1):
                own = own_row & (meta_ref[20 + sibling * 2 + v] == n)
                other = other_row & (meta_ref[20 + (1 - sibling) * 2 + v] == n)
                lanes = pl.ds(pl.multiple_of((2 * v + sibling) * TILE, TILE), TILE)
                total = total + jnp.where(own, child_ref[:, lanes], 0.0)
                total = total + jnp.where(other, came_ref[v], 0.0)
        out_ref[n * TILE : (n + 1) * TILE, :] = total.T


def assemble(meta, front, child, came):
    width = front.shape[1]
    return pl.pallas_call(
        assemble_kernel,
        grid=(1,),
        out_shape=jax.ShapeDtypeStruct((width, TILE), jnp.float32),
        in_specs=[
            pl.BlockSpec(memory_space=pltpu.SMEM),
            pl.BlockSpec((TILE, width), lambda g: (0, 0)),
            pl.BlockSpec((TILE, 4 * TILE), lambda g: (0, 0)),
            pl.BlockSpec((2, TILE, TILE), lambda g: (0, 0, 0)),
        ],
        out_specs=pl.BlockSpec((width, TILE), lambda g: (0, 0)),
        compiler_params=pltpu.CompilerParams(vmem_limit_bytes=8 * 2**20),
        name="assemble_pivot_rows",
    )(meta, front, child, came)


def body(front_init, child_blocks, tile_map):
    sibling = lax.axis_index("pair")
    row_index = lax.axis_index("row")
    col_index = lax.axis_index("col")
    half_index = col_index // 8
    column_index = sibling * 16 + col_index
    own = child_blocks[0]
    positions = tile_map.astype(jnp.int32).reshape(2, 2, 32) // 32

    with jax.named_scope("pivot_block"):
        own_positions = positions[sibling, 0]
        hit = (own_positions[row_index] == 0) & (own_positions[col_index] == 0)
        tile = jnp.where(sibling == 0, front_init[:TILE, :TILE], 0.0)
        tile = tile + jnp.where(hit, own[:TILE, :TILE], 0.0)
        upper_half, lower_half = tile[: TILE // 2], tile[TILE // 2 :]
        mine = jnp.where(half_index == 0, upper_half, 0.0)
        places = [(p, i, c) for p in range(2) for i in range(8) for c in range(8)]
        mine = (
            mine
            + lax.ppermute(upper_half, ALL, [(at(p, i, c), at(1 - p, i, c)) for p, i, c in places])
            + lax.ppermute(lower_half, ALL, [(at(p, i, c), at(p, i, c + 8)) for p, i, c in places])
            + lax.ppermute(
                lower_half, ALL, [(at(p, i, c), at(1 - p, i, c + 8)) for p, i, c in places]
            )
        )
        mine = mine[None]
        for bit in (4, 2, 1):
            came = lax.ppermute(mine, "row", [(i, i ^ bit) for i in range(8)])
            mine = jnp.concatenate([mine, came])
        mine = lax.optimization_barrier(mine)
        parts = lax.all_gather(mine, "col")

    row_positions = jnp.swapaxes(
        lax.dynamic_index_in_dim(positions.reshape(2, 2, 4, 8), row_index, 3, keepdims=False), 1, 2
    )
    column_positions = lax.dynamic_index_in_dim(positions, column_index, 2, keepdims=False)
    meta = jnp.concatenate(
        [
            jnp.stack([sibling, row_index, column_index, column_index]),
            row_positions.reshape(16),
            column_positions.reshape(4),
        ]
    ).astype(jnp.int32)

    def pick(count, v, even):
        low = own[:count, 2 * v * TILE : (2 * v + 1) * TILE]
        high = own[:count, (2 * v + 1) * TILE : 2 * (v + 1) * TILE]
        return jnp.where(even, low, high)

    with jax.named_scope("pivot_rows"):
        handed = jnp.stack([pick(TILE, v, sibling != 0) for v in range(2)])
        came = lax.ppermute(handed, "pair", SWAP)
        pivot_columns = assemble(meta, front_init, own, came)

    with jax.named_scope("panel"):
        pivot_columns, mine = lax.optimization_barrier((pivot_columns, mine))
        routes = [[], []]
        for p in range(2):
            for i in range(8):
                for c in range(16):
                    half, other = divmod(c, 8)
                    for away in range(2):
                        target = at(p ^ away, other, 8 * half + i)
                        routes[away].append((at(p, i, c), target))
        same = lax.ppermute(pivot_columns, ALL, routes[0])
        crossed = lax.ppermute(pivot_columns, ALL, routes[1])
        turned = jnp.where(
            sibling == 0, jnp.stack([same, crossed]), jnp.stack([crossed, same])
        )
        beneath = lax.all_gather(turned, "col")
        pivot_columns, turned = lax.optimization_barrier((pivot_columns, turned))
        across = ring_gather(pivot_columns)
        across, parts = lax.optimization_barrier((across, parts))

    with jax.named_scope("siblings"):
        handed = jnp.stack([pick(NPIV, v, sibling != 0) for v in range(2)])
        handed, parts = lax.optimization_barrier((handed, parts))
        received = lax.ppermute(handed, "pair", SWAP)

    with jax.named_scope("factor"):
        upper, inverse = factor(row_index, parts)
    with jax.named_scope("finish"):
        return finish(meta, front_init, own, received, across, beneath, upper, inverse)


def solution(mesh):
    return jax.shard_map(
        body,
        mesh=mesh,
        in_specs=(P("row", ("pair", "col")), P("pair", "row", "col"), P()),
        out_specs=P("row", ("pair", "col")),
        check_vma=False,
    )
```

```python
import jax
import jax.numpy as jnp
from jax import lax
from jax.experimental import pallas as pl
from jax.experimental.pallas import tpu as pltpu
from jax.sharding import PartitionSpec as P

TILE = 128
PIVOT_TILES = 8
NPIV = TILE * PIVOT_TILES
STRIP = 64
GROUP = 8
PARTS = 2
FACTOR_FLOPS = 50 * 10**9
EXACT = lax.Precision.HIGHEST


def exact_dot(a, b, contract=((1,), (0,))):
    return lax.dot_general(
        a, b, (contract, ((), ())), precision=EXACT, preferred_element_type=jnp.float32
    )


def split(x):
    parts = []
    for _ in range(PARTS):
        part = x.astype(jnp.bfloat16)
        x = x - part.astype(jnp.float32)
        parts.append(part)
    return parts


def parts_dot(a, b, contract):
    total = None
    for order in reversed(range(len(a))):
        for i in range(order + 1):
            term = lax.dot_general(
                a[i], b[order - i], (contract, ((), ())), preferred_element_type=jnp.float32
            )
            total = term if total is None else total + term
    return total


def factor_tile(block):
    row = lax.broadcasted_iota(jnp.int32, (TILE, TILE), 0)
    lane = lax.broadcasted_iota(jnp.int32, (TILE, TILE), 1)
    remaining = jnp.concatenate([block, (row == lane).astype(jnp.float32)], axis=1)
    strip_row = lax.broadcasted_iota(jnp.int32, (STRIP, TILE), 0)

    def twice(x):
        return jnp.concatenate([x, x], axis=1)

    def tall(x):
        return jnp.concatenate([x] * (STRIP // 8), axis=0)

    done = []
    for first in range(0, TILE, STRIP):
        strip = remaining[:STRIP]
        for k in range(0, STRIP, GROUP):
            at = first + k
            columns, rows, corner, inverse = [], [], {}, []
            for t in range(GROUP):
                columns.append(jnp.broadcast_to(strip[:, at + t : at + t + 1], (STRIP, TILE)))
                rows.append(jnp.broadcast_to(strip[k + t : k + t + 1], (8, 2 * TILE)))
                for r in range(t + 1):
                    corner[r, t] = jnp.broadcast_to(
                        strip[k + r : k + r + 1, at + t : at + t + 1], (8, TILE)
                    )
            for r in range(GROUP):
                inverse.append(1.0 / corner[r, r])
                for t in range(r + 1, GROUP):
                    scale = corner[r, t] * inverse[r]
                    for u in range(t, GROUP):
                        corner[t, u] = corner[t, u] - scale * corner[r, u]
                    columns[t] = columns[t] - tall(scale) * columns[r]
                    rows[t] = rows[t] - twice(scale) * rows[r]
            beneath = strip
            if k + GROUP < STRIP:
                for t in range(GROUP):
                    share = jnp.where(strip_row >= k + GROUP, columns[t] * tall(inverse[t]), 0.0)
                    beneath = beneath - twice(share) * tall(rows[t])
            for t in range(GROUP):
                root = lax.rsqrt(corner[t, t])
                root = root * (1.5 - 0.5 * corner[t, t] * root * root)
                beneath = jnp.where(
                    twice(strip_row) == k + t, tall(rows[t] * twice(root)), beneath
                )
            strip = beneath
        done.append(strip)
        if first + STRIP < TILE:
            change = exact_dot(strip[:, :TILE], strip, ((0,), (0,)))
            remaining = remaining[STRIP:] - change[first + STRIP :]
    whole = jnp.concatenate(done, axis=0)
    return jnp.where(lane >= row, whole[:, :TILE], 0.0), whole[:, TILE:]


def factor_kernel(row_ref, parts_ref, upper_ref, inverse_ref):
    for i in range(PIVOT_TILES):
        away = i ^ row_ref[0]
        place = (away & 1) * 4 + (away & 2) + (away >> 2)
        for c in range(i, PIVOT_TILES):
            for half in range(2):
                upper_ref[pl.ds(i * TILE + half * 64, 64), pl.ds(c * TILE, TILE)] = parts_ref[
                    half * 8 + c, place
                ]

    def step(j, carry):
        at = pl.ds(pl.multiple_of(j * TILE, TILE), TILE)
        upper, inverse = factor_tile(upper_ref[at, at])
        upper_ref[at, at] = upper
        inverse_ref[j] = inverse.T
        for now in range(PIVOT_TILES - 1):

            @pl.when(j == now)
            def _():
                here = slice(now * TILE, (now + 1) * TILE)
                after = slice((now + 1) * TILE, NPIV)
                solved = parts_dot(split(inverse), split(upper_ref[here, after]), ((1,), (0,)))
                upper_ref[here, after] = solved
                solved_parts = split(solved)
                for k in range(now + 1, PIVOT_TILES):
                    rows = slice(k * TILE, (k + 1) * TILE)
                    rest = slice(k * TILE, NPIV)
                    offset = (k - now - 1) * TILE
                    upper_ref[rows, rest] = upper_ref[rows, rest] - parts_dot(
                        [part[:, offset : offset + TILE] for part in solved_parts],
                        [part[:, offset:] for part in solved_parts],
                        ((0,), (0,)),
                    )

        return carry

    lax.fori_loop(0, PIVOT_TILES, step, 0)


def factor(row_index, parts):
    return pl.pallas_call(
        factor_kernel,
        out_shape=(
            jax.ShapeDtypeStruct((NPIV, NPIV), jnp.float32),
            jax.ShapeDtypeStruct((PIVOT_TILES, TILE, TILE), jnp.float32),
        ),
        in_specs=[
            pl.BlockSpec(memory_space=pltpu.SMEM),
            pl.BlockSpec(memory_space=pltpu.VMEM),
        ],
        out_specs=tuple(pl.BlockSpec(memory_space=pltpu.VMEM) for _ in range(2)),
        compiler_params=pltpu.CompilerParams(vmem_limit_bytes=24 * 2**20),
        cost_estimate=pl.CostEstimate(
            flops=FACTOR_FLOPS, bytes_accessed=9 * 2**20, transcendentals=0
        ),
        name="factor_pivots",
    )(row_index.astype(jnp.int32).reshape(1), parts)


def finish_kernel(
    meta_ref,
    front_ref,
    child_ref,
    received_ref,
    across_refs,
    beneath_ref,
    upper_ref,
    inverse_ref,
    out_ref,
    upper_parts_ref,
    wide_parts_ref,
    across_ref,
    solved_ref,
    solved_parts_ref,
):
    half_step = pl.program_id(0)
    sibling = meta_ref[0]
    row_index = meta_ref[1]
    column_index = meta_ref[2]
    width = across_ref.shape[1]
    column_rows = slice(2 * width, 3 * width)

    def solve(count, source):
        for j in range(PIVOT_TILES // 2):
            columns = slice(2 * j * TILE, 2 * (j + 1) * TILE)
            rest = jnp.concatenate([source(2 * j), source(2 * j + 1)], axis=1)
            if j:
                before = slice(0, 2 * j * TILE)
                rest = rest - parts_dot(
                    [ref[:count, before] for ref in solved_parts_ref],
                    [ref[before, columns] for ref in upper_parts_ref],
                    ((1,), (0,)),
                )
            result = parts_dot(split(rest), [ref[j] for ref in wide_parts_ref], ((1,), (0,)))
            solved_ref[:count, columns] = result
            for ref, part in zip(solved_parts_ref, split(result)):
                ref[:count, columns] = part

    def panel(i):
        return [beneath_ref[i, 0], beneath_ref[8 + i, 0]]

    @pl.when(half_step == 0)
    def _():
        for j in range(PIVOT_TILES // 2):
            rows = slice(2 * j * TILE, 2 * (j + 1) * TILE)
            after = slice(2 * (j + 1) * TILE, NPIV)
            if j < PIVOT_TILES // 2 - 1:
                for ref, part in zip(upper_parts_ref, split(upper_ref[rows, after])):
                    ref[rows, after] = part
            low, high = inverse_ref[2 * j], inverse_ref[2 * j + 1]
            between = upper_ref[
                2 * j * TILE : (2 * j + 1) * TILE, (2 * j + 1) * TILE : 2 * (j + 1) * TILE
            ]
            corner = -exact_dot(low, exact_dot(between, high))
            for ref, l, h, c in zip(wide_parts_ref, split(low), split(high), split(corner)):
                ref[j, :TILE, :TILE] = l
                ref[j, TILE:, TILE:] = h
                ref[j, :TILE, TILE:] = c
                ref[j, TILE:, :TILE] = jnp.zeros((TILE, TILE), jnp.bfloat16)

        for behind, ref in zip(RING, across_refs):
            across_ref[lax.rem(row_index - behind + 8, 8)] = ref[...]
        solve(3 * width, lambda i: jnp.concatenate(panel(i) + [across_ref[i]]))

    @pl.when(half_step > 0)
    def _():
        solve(2 * width, lambda i: jnp.concatenate(panel(i)))

    update = parts_dot(
        [ref[: 2 * width] for ref in solved_parts_ref],
        [ref[column_rows] for ref in solved_parts_ref],
        ((1,), (1,)),
    )

    for half in range(2):
        group = 2 * half_step + half

        def row_slot(s, u):
            return meta_ref[4 + s * 8 + group * 2 + u]

        def column_slot(s, u):
            return meta_ref[20 + s * 2 + u]

        for m in range(3):
            for n in range(3):
                lanes = slice(n * TILE, (n + 1) * TILE)
                total = front_ref[m, half, :, lanes]
                for u in range(2):
                    for v in range(2):
                        if m - u in (0, 1) and n - v in (0, 1):
                            own = (row_slot(sibling, u) == m) & (column_slot(sibling, v) == n)
                            other = (row_slot(1 - sibling, u) == m) & (
                                column_slot(1 - sibling, v) == n
                            )
                            own_lanes = pl.ds(
                                pl.multiple_of((2 * v + sibling) * TILE, TILE), TILE
                            )
                            mine = child_ref[u, half, :, own_lanes]
                            theirs = received_ref[v, u, half]
                            total = total + jnp.where(own, mine, 0.0)
                            total = total + jnp.where(other, theirs, 0.0)
                top = half * width + m * TILE
                out_ref[m, half, :, lanes] = (
                    total - update[top : top + TILE, n * TILE : (n + 1) * TILE]
                )

    pivot_column = column_index < PIVOT_TILES
    own_column = pl.ds(pl.multiple_of(lax.rem(column_index, 8) * TILE, TILE), TILE)

    @pl.when(pivot_column)
    def _():
        for half in range(2):
            for m in range(3):
                top = half * width + m * TILE
                out_ref[m, half, :, :TILE] = solved_ref[top : top + TILE, own_column]

    @pl.when(half_step == 0)
    def _():
        own_row = pl.ds(pl.multiple_of(row_index * TILE, TILE), TILE)
        for n in range(3):
            lanes = slice(n * TILE, (n + 1) * TILE)
            top = 2 * width + n * TILE
            out_ref[0, 0, :, lanes] = solved_ref[top : top + TILE, own_row].T

        @pl.when(pivot_column)
        def _():
            @pl.when(row_index < column_index)
            def _():
                out_ref[0, 0, :, :TILE] = upper_ref[own_row, own_column]

            @pl.when(row_index > column_index)
            def _():
                out_ref[0, 0, :, :TILE] = upper_ref[own_column, own_row].T

            @pl.when(row_index == column_index)
            def _():
                row = lax.broadcasted_iota(jnp.int32, (TILE, TILE), 0)
                lane = lax.broadcasted_iota(jnp.int32, (TILE, TILE), 1)
                tile = upper_ref[own_row, own_column]
                out_ref[0, 0, :, :TILE] = jnp.where(row > lane, tile.T, tile)


def finish(meta, front, child, received, across, beneath, upper, inverse):
    width = front.shape[1]
    whole = pl.BlockSpec(memory_space=pltpu.VMEM)
    held = lambda *shape: [pltpu.VMEM(shape, jnp.bfloat16) for _ in range(PARTS)]
    out = pl.pallas_call(
        finish_kernel,
        grid=(2,),
        out_shape=jax.ShapeDtypeStruct((3, 4, TILE, width), jnp.float32),
        in_specs=[
            pl.BlockSpec(memory_space=pltpu.SMEM),
            pl.BlockSpec((3, 2, TILE, width), lambda g: (0, g, 0, 0)),
            pl.BlockSpec((2, 2, TILE, 4 * TILE), lambda g: (0, g, 0, 0)),
            pl.BlockSpec((2, 2, 2, TILE, TILE), lambda g: (0, 0, g, 0, 0)),
            [whole] * 8,
            pl.BlockSpec((16, 1, width, TILE), lambda g: (0, g, 0, 0)),
            whole,
            whole,
        ],
        out_specs=pl.BlockSpec((3, 2, TILE, width), lambda g: (0, g, 0, 0)),
        scratch_shapes=[
            held(NPIV, NPIV),
            held(PIVOT_TILES // 2, 2 * TILE, 2 * TILE),
            pltpu.VMEM((8, width, TILE), jnp.float32),
            pltpu.VMEM((3 * width, NPIV), jnp.float32),
            held(3 * width, NPIV),
        ],
        compiler_params=pltpu.CompilerParams(vmem_limit_bytes=50 * 2**20),
        cost_estimate=pl.CostEstimate(
            flops=15 * 10**9, bytes_accessed=24 * 2**20, transcendentals=0
        ),
        name="solve_and_update",
    )(
        meta,
        front.reshape(3, 4, TILE, width),
        child.reshape(2, 4, TILE, 4 * TILE),
        received.reshape(2, 2, 4, TILE, TILE),
        across,
        beneath,
        upper,
        inverse,
    )
    return out.reshape(front.shape)


ALL = ("pair", "row", "col")
SWAP = [(0, 1), (1, 0)]
RING = (0, 1, 7, 2, 6, 3, 5, 4)


def at(pair, row, col):
    return (pair * 8 + row) * 16 + col


def ring_gather(block):
    up = [(i, (i + 1) % 8) for i in range(8)]
    down = [(i, (i - 1) % 8) for i in range(8)]
    half = block.shape[0] // 2
    behind = ahead = block
    blocks = [block]
    for _ in range(3):
        behind = lax.ppermute(behind, "row", up)
        ahead = lax.ppermute(ahead, "row", down)
        blocks += [behind, ahead]
    last = [lax.ppermute(behind[:half], "row", up), lax.ppermute(ahead[half:], "row", down)]
    return blocks + [jnp.concatenate(last)]


def assemble_kernel(meta_ref, front_ref, child_ref, came_ref, out_ref):
    sibling = meta_ref[0]
    own_row = meta_ref[4 + sibling * 8] == 0
    other_row = meta_ref[4 + (1 - sibling) * 8] == 0
    for n in range(3):
        total = front_ref[:, n * TILE : (n + 1) * TILE]
        for v in range(2):
            if n - v in (0, 1):
                own = own_row & (meta_ref[20 + sibling * 2 + v] == n)
                other = other_row & (meta_ref[20 + (1 - sibling) * 2 + v] == n)
                lanes = pl.ds(pl.multiple_of((2 * v + sibling) * TILE, TILE), TILE)
                total = total + jnp.where(own, child_ref[:, lanes], 0.0)
                total = total + jnp.where(other, came_ref[v], 0.0)
        out_ref[n * TILE : (n + 1) * TILE, :] = total.T


def assemble(meta, front, child, came):
    width = front.shape[1]
    return pl.pallas_call(
        assemble_kernel,
        grid=(1,),
        out_shape=jax.ShapeDtypeStruct((width, TILE), jnp.float32),
        in_specs=[
            pl.BlockSpec(memory_space=pltpu.SMEM),
            pl.BlockSpec((TILE, width), lambda g: (0, 0)),
            pl.BlockSpec((TILE, 4 * TILE), lambda g: (0, 0)),
            pl.BlockSpec((2, TILE, TILE), lambda g: (0, 0, 0)),
        ],
        out_specs=pl.BlockSpec((width, TILE), lambda g: (0, 0)),
        compiler_params=pltpu.CompilerParams(vmem_limit_bytes=8 * 2**20),
        name="assemble_pivot_rows",
    )(meta, front, child, came)


def body(front_init, child_blocks, tile_map):
    sibling = lax.axis_index("pair")
    row_index = lax.axis_index("row")
    col_index = lax.axis_index("col")
    half_index = col_index // 8
    column_index = sibling * 16 + col_index
    own = child_blocks[0]
    positions = tile_map.astype(jnp.int32).reshape(2, 2, 32) // 32

    def pick(count, v, even):
        low = own[:count, 2 * v * TILE : (2 * v + 1) * TILE]
        high = own[:count, (2 * v + 1) * TILE : 2 * (v + 1) * TILE]
        return jnp.where(even, low, high)

    with jax.named_scope("pivot_block"):
        own_positions = positions[sibling, 0]
        hit = (own_positions[row_index] == 0) & (own_positions[col_index] == 0)
        tile = jnp.where(sibling == 0, front_init[:TILE, :TILE], 0.0)
        tile = tile + jnp.where(hit, own[:TILE, :TILE], 0.0)
        upper_half, lower_half = tile[: TILE // 2], tile[TILE // 2 :]
        mine = jnp.where(half_index == 0, upper_half, 0.0)
        places = [(p, i, c) for p in range(2) for i in range(8) for c in range(8)]
        mine = (
            mine
            + lax.ppermute(upper_half, ALL, [(at(p, i, c), at(1 - p, i, c)) for p, i, c in places])
            + lax.ppermute(lower_half, ALL, [(at(p, i, c), at(p, i, c + 8)) for p, i, c in places])
            + lax.ppermute(
                lower_half, ALL, [(at(p, i, c), at(1 - p, i, c + 8)) for p, i, c in places]
            )
        )
    with jax.named_scope("siblings"):
        first = jnp.stack([pick(TILE, v, sibling != 0) for v in range(2)])
        first = lax.ppermute(first, "pair", SWAP)
        handed = jnp.stack([pick(NPIV, v, sibling != 0) for v in range(2)])
        handed, mine = lax.optimization_barrier((handed, mine))
        received = lax.ppermute(handed, "pair", SWAP)

    with jax.named_scope("pivot_gather"):
        mine = mine[None]
        for bit in (4, 2, 1):
            came = lax.ppermute(mine, "row", [(i, i ^ bit) for i in range(8)])
            mine = jnp.concatenate([mine, came])
            if bit == 2:
                mine, first = lax.optimization_barrier((mine, first))
        parts = lax.all_gather(mine, "col")

    row_positions = jnp.swapaxes(
        lax.dynamic_index_in_dim(positions.reshape(2, 2, 4, 8), row_index, 3, keepdims=False), 1, 2
    )
    column_positions = lax.dynamic_index_in_dim(positions, column_index, 2, keepdims=False)
    meta = jnp.concatenate(
        [
            jnp.stack([sibling, row_index, column_index, column_index]),
            row_positions.reshape(16),
            column_positions.reshape(4),
        ]
    ).astype(jnp.int32)

    with jax.named_scope("pivot_rows"):
        pivot_columns = assemble(meta, front_init, own, first)

    with jax.named_scope("panel"):
        pivot_columns, mine = lax.optimization_barrier((pivot_columns, mine))
        routes = [[], []]
        for p in range(2):
            for i in range(8):
                for c in range(16):
                    half, other = divmod(c, 8)
                    for away in range(2):
                        target = at(p ^ away, other, 8 * half + i)
                        routes[away].append((at(p, i, c), target))
        same = lax.ppermute(pivot_columns, ALL, routes[0])
        crossed = lax.ppermute(pivot_columns, ALL, routes[1])
        turned = jnp.where(
            sibling == 0, jnp.stack([same, crossed]), jnp.stack([crossed, same])
        )
        beneath = lax.all_gather(turned, "col")
        pivot_columns, turned, received = lax.optimization_barrier(
            (pivot_columns, turned, received)
        )
        across = ring_gather(pivot_columns)
        across, parts = lax.optimization_barrier((across, parts))

    with jax.named_scope("factor"):
        upper, inverse = factor(row_index, parts)
    with jax.named_scope("finish"):
        return finish(meta, front_init, own, received, across, beneath, upper, inverse)


def solution(mesh):
    return jax.shard_map(
        body,
        mesh=mesh,
        in_specs=(P("row", ("pair", "col")), P("pair", "row", "col"), P()),
        out_specs=P("row", ("pair", "col")),
        check_vma=False,
    )
```

```python
import jax
import jax.numpy as jnp
from jax import lax
from jax.experimental import pallas as pl
from jax.experimental.pallas import tpu as pltpu
from jax.sharding import PartitionSpec as P

TILE = 128
PIVOT_TILES = 8
NPIV = TILE * PIVOT_TILES
STRIP = 64
GROUP = 8
PARTS = 2
FACTOR_FLOPS = 50 * 10**9
EXACT = lax.Precision.HIGHEST


def exact_dot(a, b, contract=((1,), (0,))):
    return lax.dot_general(
        a, b, (contract, ((), ())), precision=EXACT, preferred_element_type=jnp.float32
    )


def split(x):
    parts = []
    for _ in range(PARTS):
        part = x.astype(jnp.bfloat16)
        x = x - part.astype(jnp.float32)
        parts.append(part)
    return parts


def parts_dot(a, b, contract):
    total = None
    for order in reversed(range(len(a))):
        for i in range(order + 1):
            term = lax.dot_general(
                a[i], b[order - i], (contract, ((), ())), preferred_element_type=jnp.float32
            )
            total = term if total is None else total + term
    return total


def factor_tile(block):
    row = lax.broadcasted_iota(jnp.int32, (TILE, TILE), 0)
    lane = lax.broadcasted_iota(jnp.int32, (TILE, TILE), 1)
    remaining = jnp.concatenate([block, (row == lane).astype(jnp.float32)], axis=1)
    strip_row = lax.broadcasted_iota(jnp.int32, (STRIP, TILE), 0)

    def twice(x):
        return jnp.concatenate([x, x], axis=1)

    def tall(x):
        return jnp.concatenate([x] * (STRIP // 8), axis=0)

    done = []
    for first in range(0, TILE, STRIP):
        strip = remaining[:STRIP]
        for k in range(0, STRIP, GROUP):
            at = first + k
            columns, rows, corner, inverse = [], [], {}, []
            for t in range(GROUP):
                columns.append(jnp.broadcast_to(strip[:, at + t : at + t + 1], (STRIP, TILE)))
                rows.append(jnp.broadcast_to(strip[k + t : k + t + 1], (8, 2 * TILE)))
                for r in range(t + 1):
                    corner[r, t] = jnp.broadcast_to(
                        strip[k + r : k + r + 1, at + t : at + t + 1], (8, TILE)
                    )
            for r in range(GROUP):
                inverse.append(1.0 / corner[r, r])
                for t in range(r + 1, GROUP):
                    scale = corner[r, t] * inverse[r]
                    for u in range(t, GROUP):
                        corner[t, u] = corner[t, u] - scale * corner[r, u]
                    columns[t] = columns[t] - tall(scale) * columns[r]
                    rows[t] = rows[t] - twice(scale) * rows[r]
            beneath = strip
            if k + GROUP < STRIP:
                for t in range(GROUP):
                    share = jnp.where(strip_row >= k + GROUP, columns[t] * tall(inverse[t]), 0.0)
                    beneath = beneath - twice(share) * tall(rows[t])
            for t in range(GROUP):
                root = lax.rsqrt(corner[t, t])
                root = root * (1.5 - 0.5 * corner[t, t] * root * root)
                beneath = jnp.where(
                    twice(strip_row) == k + t, tall(rows[t] * twice(root)), beneath
                )
            strip = beneath
        done.append(strip)
        if first + STRIP < TILE:
            change = exact_dot(strip[:, :TILE], strip, ((0,), (0,)))
            remaining = remaining[STRIP:] - change[first + STRIP :]
    whole = jnp.concatenate(done, axis=0)
    return jnp.where(lane >= row, whole[:, :TILE], 0.0), whole[:, TILE:]


def factor_kernel(row_ref, parts_ref, upper_ref, inverse_ref):
    for i in range(PIVOT_TILES):
        away = i ^ row_ref[0]
        place = (away & 1) * 4 + (away & 2) + (away >> 2)
        for c in range(i, PIVOT_TILES):
            for half in range(2):
                upper_ref[pl.ds(i * TILE + half * 64, 64), pl.ds(c * TILE, TILE)] = parts_ref[
                    half * 8 + c, place
                ]

    def step(j, carry):
        at = pl.ds(pl.multiple_of(j * TILE, TILE), TILE)
        upper, inverse = factor_tile(upper_ref[at, at])
        upper_ref[at, at] = upper
        inverse_ref[j] = inverse.T
        for now in range(PIVOT_TILES - 1):

            @pl.when(j == now)
            def _():
                here = slice(now * TILE, (now + 1) * TILE)
                after = slice((now + 1) * TILE, NPIV)
                solved = parts_dot(split(inverse), split(upper_ref[here, after]), ((1,), (0,)))
                upper_ref[here, after] = solved
                solved_parts = split(solved)
                for k in range(now + 1, PIVOT_TILES):
                    rows = slice(k * TILE, (k + 1) * TILE)
                    rest = slice(k * TILE, NPIV)
                    offset = (k - now - 1) * TILE
                    upper_ref[rows, rest] = upper_ref[rows, rest] - parts_dot(
                        [part[:, offset : offset + TILE] for part in solved_parts],
                        [part[:, offset:] for part in solved_parts],
                        ((0,), (0,)),
                    )

        return carry

    lax.fori_loop(0, PIVOT_TILES, step, 0)


def factor(row_index, parts):
    return pl.pallas_call(
        factor_kernel,
        out_shape=(
            jax.ShapeDtypeStruct((NPIV, NPIV), jnp.float32),
            jax.ShapeDtypeStruct((PIVOT_TILES, TILE, TILE), jnp.float32),
        ),
        in_specs=[
            pl.BlockSpec(memory_space=pltpu.SMEM),
            pl.BlockSpec(memory_space=pltpu.VMEM),
        ],
        out_specs=tuple(pl.BlockSpec(memory_space=pltpu.VMEM) for _ in range(2)),
        compiler_params=pltpu.CompilerParams(vmem_limit_bytes=24 * 2**20),
        cost_estimate=pl.CostEstimate(
            flops=FACTOR_FLOPS, bytes_accessed=9 * 2**20, transcendentals=0
        ),
        name="factor_pivots",
    )(row_index.astype(jnp.int32).reshape(1), parts)


def finish_kernel(
    meta_ref,
    front_ref,
    child_ref,
    received_ref,
    across_refs,
    beneath_ref,
    upper_ref,
    inverse_ref,
    out_ref,
    upper_parts_ref,
    wide_parts_ref,
    across_ref,
    solved_ref,
    solved_parts_ref,
):
    half_step = pl.program_id(0)
    sibling = meta_ref[0]
    row_index = meta_ref[1]
    column_index = meta_ref[2]
    width = across_ref.shape[1]
    column_rows = slice(2 * width, 3 * width)

    def solve(count, source):
        for j in range(PIVOT_TILES // 2):
            columns = slice(2 * j * TILE, 2 * (j + 1) * TILE)
            rest = jnp.concatenate([source(2 * j), source(2 * j + 1)], axis=1)
            if j:
                before = slice(0, 2 * j * TILE)
                rest = rest - parts_dot(
                    [ref[:count, before] for ref in solved_parts_ref],
                    [ref[before, columns] for ref in upper_parts_ref],
                    ((1,), (0,)),
                )
            result = parts_dot(split(rest), [ref[j] for ref in wide_parts_ref], ((1,), (0,)))
            solved_ref[:count, columns] = result
            for ref, part in zip(solved_parts_ref, split(result)):
                ref[:count, columns] = part

    def panel(i):
        return [beneath_ref[i, 0], beneath_ref[8 + i, 0]]

    @pl.when(half_step == 0)
    def _():
        for j in range(PIVOT_TILES // 2):
            rows = slice(2 * j * TILE, 2 * (j + 1) * TILE)
            after = slice(2 * (j + 1) * TILE, NPIV)
            if j < PIVOT_TILES // 2 - 1:
                for ref, part in zip(upper_parts_ref, split(upper_ref[rows, after])):
                    ref[rows, after] = part
            low, high = inverse_ref[2 * j], inverse_ref[2 * j + 1]
            between = upper_ref[
                2 * j * TILE : (2 * j + 1) * TILE, (2 * j + 1) * TILE : 2 * (j + 1) * TILE
            ]
            corner = -exact_dot(low, exact_dot(between, high))
            for ref, l, h, c in zip(wide_parts_ref, split(low), split(high), split(corner)):
                ref[j, :TILE, :TILE] = l
                ref[j, TILE:, TILE:] = h
                ref[j, :TILE, TILE:] = c
                ref[j, TILE:, :TILE] = jnp.zeros((TILE, TILE), jnp.bfloat16)

        for behind, ref in zip(RING, across_refs):
            across_ref[lax.rem(row_index - behind + 8, 8)] = ref[...]
        solve(3 * width, lambda i: jnp.concatenate(panel(i) + [across_ref[i]]))

    @pl.when(half_step > 0)
    def _():
        solve(2 * width, lambda i: jnp.concatenate(panel(i)))

    update = parts_dot(
        [ref[: 2 * width] for ref in solved_parts_ref],
        [ref[column_rows] for ref in solved_parts_ref],
        ((1,), (1,)),
    )

    for half in range(2):
        group = 2 * half_step + half

        def row_slot(s, u):
            return meta_ref[4 + s * 8 + group * 2 + u]

        def column_slot(s, u):
            return meta_ref[20 + s * 2 + u]

        for m in range(3):
            for n in range(3):
                lanes = slice(n * TILE, (n + 1) * TILE)
                total = front_ref[m, half, :, lanes]
                for u in range(2):
                    for v in range(2):
                        if m - u in (0, 1) and n - v in (0, 1):
                            own = (row_slot(sibling, u) == m) & (column_slot(sibling, v) == n)
                            other = (row_slot(1 - sibling, u) == m) & (
                                column_slot(1 - sibling, v) == n
                            )
                            own_lanes = pl.ds(
                                pl.multiple_of((2 * v + sibling) * TILE, TILE), TILE
                            )
                            mine = child_ref[u, half, :, own_lanes]
                            theirs = received_ref[v, u, half]
                            total = total + jnp.where(own, mine, 0.0)
                            total = total + jnp.where(other, theirs, 0.0)
                top = half * width + m * TILE
                out_ref[m, half, :, lanes] = (
                    total - update[top : top + TILE, n * TILE : (n + 1) * TILE]
                )

    pivot_column = column_index < PIVOT_TILES
    own_column = pl.ds(pl.multiple_of(lax.rem(column_index, 8) * TILE, TILE), TILE)

    @pl.when(pivot_column)
    def _():
        for half in range(2):
            for m in range(3):
                top = half * width + m * TILE
                out_ref[m, half, :, :TILE] = solved_ref[top : top + TILE, own_column]

    @pl.when(half_step == 0)
    def _():
        own_row = pl.ds(pl.multiple_of(row_index * TILE, TILE), TILE)
        for n in range(3):
            lanes = slice(n * TILE, (n + 1) * TILE)
            top = 2 * width + n * TILE
            out_ref[0, 0, :, lanes] = solved_ref[top : top + TILE, own_row].T

        @pl.when(pivot_column)
        def _():
            @pl.when(row_index < column_index)
            def _():
                out_ref[0, 0, :, :TILE] = upper_ref[own_row, own_column]

            @pl.when(row_index > column_index)
            def _():
                out_ref[0, 0, :, :TILE] = upper_ref[own_column, own_row].T

            @pl.when(row_index == column_index)
            def _():
                row = lax.broadcasted_iota(jnp.int32, (TILE, TILE), 0)
                lane = lax.broadcasted_iota(jnp.int32, (TILE, TILE), 1)
                tile = upper_ref[own_row, own_column]
                out_ref[0, 0, :, :TILE] = jnp.where(row > lane, tile.T, tile)


def finish(meta, front, child, received, across, beneath, upper, inverse):
    width = front.shape[1]
    whole = pl.BlockSpec(memory_space=pltpu.VMEM)
    held = lambda *shape: [pltpu.VMEM(shape, jnp.bfloat16) for _ in range(PARTS)]
    out = pl.pallas_call(
        finish_kernel,
        grid=(2,),
        out_shape=jax.ShapeDtypeStruct((3, 4, TILE, width), jnp.float32),
        in_specs=[
            pl.BlockSpec(memory_space=pltpu.SMEM),
            pl.BlockSpec((3, 2, TILE, width), lambda g: (0, g, 0, 0)),
            pl.BlockSpec((2, 2, TILE, 4 * TILE), lambda g: (0, g, 0, 0)),
            pl.BlockSpec((2, 2, 2, TILE, TILE), lambda g: (0, 0, g, 0, 0)),
            [whole] * 8,
            pl.BlockSpec((16, 1, width, TILE), lambda g: (0, g, 0, 0)),
            whole,
            whole,
        ],
        out_specs=pl.BlockSpec((3, 2, TILE, width), lambda g: (0, g, 0, 0)),
        scratch_shapes=[
            held(NPIV, NPIV),
            held(PIVOT_TILES // 2, 2 * TILE, 2 * TILE),
            pltpu.VMEM((8, width, TILE), jnp.float32),
            pltpu.VMEM((3 * width, NPIV), jnp.float32),
            held(3 * width, NPIV),
        ],
        compiler_params=pltpu.CompilerParams(vmem_limit_bytes=50 * 2**20),
        cost_estimate=pl.CostEstimate(
            flops=15 * 10**9, bytes_accessed=24 * 2**20, transcendentals=0
        ),
        name="solve_and_update",
    )(
        meta,
        front.reshape(3, 4, TILE, width),
        child.reshape(2, 4, TILE, 4 * TILE),
        received.reshape(2, 2, 4, TILE, TILE),
        across,
        beneath,
        upper,
        inverse,
    )
    return out.reshape(front.shape)


ALL = ("pair", "row", "col")
SWAP = [(0, 1), (1, 0)]
RING = (0, 1, 7, 2, 6, 3, 5, 4)


def at(pair, row, col):
    return (pair * 8 + row) * 16 + col


def ring_gather(block, beside):
    up = [(i, (i + 1) % 8) for i in range(8)]
    down = [(i, (i - 1) % 8) for i in range(8)]
    half = block.shape[0] // 2
    behind = ahead = block
    blocks = [block]
    for turn in range(3):
        behind = lax.ppermute(behind, "row", up)
        ahead = lax.ppermute(ahead, "row", down)
        if turn < len(beside):
            behind, ahead, beside[turn] = lax.optimization_barrier((behind, ahead, beside[turn]))
        blocks += [behind, ahead]
    last = [lax.ppermute(behind[:half], "row", up), lax.ppermute(ahead[half:], "row", down)]
    return blocks + [jnp.concatenate(last)]


def assemble_kernel(meta_ref, front_ref, child_ref, came_ref, out_ref):
    sibling = meta_ref[0]
    own_row = meta_ref[4 + sibling * 8] == 0
    other_row = meta_ref[4 + (1 - sibling) * 8] == 0
    for n in range(3):
        total = front_ref[:, n * TILE : (n + 1) * TILE]
        for v in range(2):
            if n - v in (0, 1):
                own = own_row & (meta_ref[20 + sibling * 2 + v] == n)
                other = other_row & (meta_ref[20 + (1 - sibling) * 2 + v] == n)
                lanes = pl.ds(pl.multiple_of((2 * v + sibling) * TILE, TILE), TILE)
                total = total + jnp.where(own, child_ref[:, lanes], 0.0)
                total = total + jnp.where(other, came_ref[v], 0.0)
        out_ref[n * TILE : (n + 1) * TILE, :] = total.T


def assemble(meta, front, child, came):
    width = front.shape[1]
    return pl.pallas_call(
        assemble_kernel,
        grid=(1,),
        out_shape=jax.ShapeDtypeStruct((width, TILE), jnp.float32),
        in_specs=[
            pl.BlockSpec(memory_space=pltpu.SMEM),
            pl.BlockSpec((TILE, width), lambda g: (0, 0)),
            pl.BlockSpec((TILE, 4 * TILE), lambda g: (0, 0)),
            pl.BlockSpec((2, TILE, TILE), lambda g: (0, 0, 0)),
        ],
        out_specs=pl.BlockSpec((width, TILE), lambda g: (0, 0)),
        compiler_params=pltpu.CompilerParams(vmem_limit_bytes=8 * 2**20),
        name="assemble_pivot_rows",
    )(meta, front, child, came)


def body(front_init, child_blocks, tile_map):
    sibling = lax.axis_index("pair")
    row_index = lax.axis_index("row")
    col_index = lax.axis_index("col")
    half_index = col_index // 8
    column_index = sibling * 16 + col_index
    own = child_blocks[0]
    positions = tile_map.astype(jnp.int32).reshape(2, 2, 32) // 32

    def pick(count, v, even):
        low = own[:count, 2 * v * TILE : (2 * v + 1) * TILE]
        high = own[:count, (2 * v + 1) * TILE : 2 * (v + 1) * TILE]
        return jnp.where(even, low, high)

    with jax.named_scope("pivot_block"):
        own_positions = positions[sibling, 0]
        hit = (own_positions[row_index] == 0) & (own_positions[col_index] == 0)
        tile = jnp.where(sibling == 0, front_init[:TILE, :TILE], 0.0)
        tile = tile + jnp.where(hit, own[:TILE, :TILE], 0.0)
        upper_half, lower_half = tile[: TILE // 2], tile[TILE // 2 :]
        mine = jnp.where(half_index == 0, upper_half, 0.0)
        places = [(p, i, c) for p in range(2) for i in range(8) for c in range(8)]
        mine = (
            mine
            + lax.ppermute(upper_half, ALL, [(at(p, i, c), at(1 - p, i, c)) for p, i, c in places])
            + lax.ppermute(lower_half, ALL, [(at(p, i, c), at(p, i, c + 8)) for p, i, c in places])
            + lax.ppermute(
                lower_half, ALL, [(at(p, i, c), at(1 - p, i, c + 8)) for p, i, c in places]
            )
        )
    with jax.named_scope("siblings"):
        handed = jnp.stack([pick(NPIV, v, sibling != 0) for v in range(2)])
        handed, mine = lax.optimization_barrier((handed, mine))
        received = lax.ppermute(handed, "pair", SWAP)

    with jax.named_scope("pivot_gather"):
        mine = mine[None]
        for bit in (4, 2, 1):
            came = lax.ppermute(mine, "row", [(i, i ^ bit) for i in range(8)])
            mine = jnp.concatenate([mine, came])
        mine, received = lax.optimization_barrier((mine, received))
        parts = lax.all_gather(mine, "col")

    row_positions = jnp.swapaxes(
        lax.dynamic_index_in_dim(positions.reshape(2, 2, 4, 8), row_index, 3, keepdims=False), 1, 2
    )
    column_positions = lax.dynamic_index_in_dim(positions, column_index, 2, keepdims=False)
    meta = jnp.concatenate(
        [
            jnp.stack([sibling, row_index, column_index, column_index]),
            row_positions.reshape(16),
            column_positions.reshape(4),
        ]
    ).astype(jnp.int32)

    with jax.named_scope("pivot_rows"):
        pivot_columns = assemble(meta, front_init, own, received)

    with jax.named_scope("panel"):
        pivot_columns, mine = lax.optimization_barrier((pivot_columns, mine))
        routes = [[], []]
        for p in range(2):
            for i in range(8):
                for c in range(16):
                    half, other = divmod(c, 8)
                    for away in range(2):
                        target = at(p ^ away, other, 8 * half + i)
                        routes[away].append((at(p, i, c), target))
        beside = [lax.ppermute(pivot_columns, ALL, route) for route in routes]
        across = ring_gather(pivot_columns, beside)
        same, crossed = beside
        turned = jnp.where(
            sibling == 0, jnp.stack([same, crossed]), jnp.stack([crossed, same])
        )
        beneath = lax.all_gather(turned, "col")
        across, parts = lax.optimization_barrier((across, parts))

    with jax.named_scope("factor"):
        upper, inverse = factor(row_index, parts)
    with jax.named_scope("finish"):
        return finish(meta, front_init, own, received, across, beneath, upper, inverse)


def solution(mesh):
    return jax.shard_map(
        body,
        mesh=mesh,
        in_specs=(P("row", ("pair", "col")), P("pair", "row", "col"), P()),
        out_specs=P("row", ("pair", "col")),
        check_vma=False,
    )
```

```python
import jax
import jax.numpy as jnp
from jax import lax
from jax.experimental import pallas as pl
from jax.experimental.pallas import tpu as pltpu
from jax.sharding import PartitionSpec as P

TILE = 128
PIVOT_TILES = 8
NPIV = TILE * PIVOT_TILES
STRIP = 64
GROUP = 8
PARTS = 2
FACTOR_FLOPS = 50 * 10**9
EXACT = lax.Precision.HIGHEST


def exact_dot(a, b, contract=((1,), (0,))):
    return lax.dot_general(
        a, b, (contract, ((), ())), precision=EXACT, preferred_element_type=jnp.float32
    )


def split(x):
    parts = []
    for _ in range(PARTS):
        part = x.astype(jnp.bfloat16)
        x = x - part.astype(jnp.float32)
        parts.append(part)
    return parts


def parts_dot(a, b, contract):
    pairs = [(i, order - i) for order in range(len(a)) for i in range(order + 1)]
    return lax.dot_general(
        jnp.concatenate([a[i] for i, _ in pairs], axis=contract[0][0]),
        jnp.concatenate([b[j] for _, j in pairs], axis=contract[1][0]),
        (contract, ((), ())),
        preferred_element_type=jnp.float32,
    )


def factor_tile(block):
    row = lax.broadcasted_iota(jnp.int32, (TILE, TILE), 0)
    lane = lax.broadcasted_iota(jnp.int32, (TILE, TILE), 1)
    remaining = jnp.concatenate([block, (row == lane).astype(jnp.float32)], axis=1)
    group_row = lax.broadcasted_iota(jnp.int32, (GROUP, 2 * TILE), 0)

    def twice(x):
        return jnp.concatenate([x, x], axis=1)

    def tall(x, count):
        return jnp.concatenate([x] * (count // GROUP), axis=0)

    done = []
    for first in range(0, TILE, STRIP):
        strip = remaining[:STRIP]
        finished = []
        for k in range(0, STRIP, GROUP):
            at = first + k
            count = STRIP - k - GROUP
            top, beneath = strip[:GROUP], strip[GROUP:]
            columns, rows, corner, inverse = [], [], {}, []
            for t in range(GROUP):
                if count:
                    columns.append(jnp.broadcast_to(beneath[:, at + t : at + t + 1], (count, TILE)))
                rows.append(jnp.broadcast_to(top[t : t + 1], (GROUP, 2 * TILE)))
                for r in range(t + 1):
                    corner[r, t] = jnp.broadcast_to(
                        top[r : r + 1, at + t : at + t + 1], (GROUP, TILE)
                    )
            for r in range(GROUP):
                inverse.append(1.0 / corner[r, r])
                for t in range(r + 1, GROUP):
                    scale = corner[r, t] * inverse[r]
                    for u in range(t, GROUP):
                        product = corner[r, t] * corner[r, u]
                        corner[t, u] = corner[t, u] - product * inverse[r]
                    if count:
                        columns[t] = columns[t] - tall(scale, count) * columns[r]
                    rows[t] = rows[t] - twice(scale) * rows[r]
            if count:
                for t in range(GROUP):
                    share = columns[t] * tall(inverse[t], count)
                    beneath = beneath - twice(share) * tall(rows[t], count)
            result = None
            for t in range(GROUP):
                root = lax.rsqrt(corner[t, t])
                root = root * (1.5 - 0.5 * corner[t, t] * root * root)
                scaled = rows[t] * twice(root)
                result = scaled if t == 0 else jnp.where(group_row == t, scaled, result)
            finished.append(result)
            strip = beneath
        strip = jnp.concatenate(finished, axis=0)
        done.append(strip)
        if first + STRIP < TILE:
            change = exact_dot(strip[:, :TILE], strip, ((0,), (0,)))
            remaining = remaining[STRIP:] - change[first + STRIP :]
    whole = jnp.concatenate(done, axis=0)
    return jnp.where(lane >= row, whole[:, :TILE], 0.0), whole[:, TILE:]


def factor_kernel(row_ref, parts_ref, upper_ref, inverse_ref):
    for i in range(PIVOT_TILES):
        away = i ^ row_ref[0]
        place = (away & 1) * 4 + (away & 2) + (away >> 2)
        for c in range(i, PIVOT_TILES):
            for half in range(2):
                upper_ref[pl.ds(i * TILE + half * 64, 64), pl.ds(c * TILE, TILE)] = parts_ref[
                    half * 8 + c, place
                ]

    def step(j, carry):
        at = pl.ds(pl.multiple_of(j * TILE, TILE), TILE)
        upper, inverse = factor_tile(upper_ref[at, at])
        upper_ref[at, at] = upper
        inverse_ref[j] = inverse.T
        for now in range(PIVOT_TILES - 1):

            @pl.when(j == now)
            def _():
                here = slice(now * TILE, (now + 1) * TILE)
                after = slice((now + 1) * TILE, NPIV)
                solved = parts_dot(split(inverse), split(upper_ref[here, after]), ((1,), (0,)))
                upper_ref[here, after] = solved
                solved_parts = split(solved)
                for k in range(now + 1, PIVOT_TILES):
                    rows = slice(k * TILE, (k + 1) * TILE)
                    rest = slice(k * TILE, NPIV)
                    offset = (k - now - 1) * TILE
                    upper_ref[rows, rest] = upper_ref[rows, rest] - parts_dot(
                        [part[:, offset : offset + TILE] for part in solved_parts],
                        [part[:, offset:] for part in solved_parts],
                        ((0,), (0,)),
                    )

        return carry

    lax.fori_loop(0, PIVOT_TILES, step, 0)


def factor(row_index, parts):
    return pl.pallas_call(
        factor_kernel,
        out_shape=(
            jax.ShapeDtypeStruct((NPIV, NPIV), jnp.float32),
            jax.ShapeDtypeStruct((PIVOT_TILES, TILE, TILE), jnp.float32),
        ),
        in_specs=[
            pl.BlockSpec(memory_space=pltpu.SMEM),
            pl.BlockSpec(memory_space=pltpu.VMEM),
        ],
        out_specs=tuple(pl.BlockSpec(memory_space=pltpu.VMEM) for _ in range(2)),
        compiler_params=pltpu.CompilerParams(vmem_limit_bytes=24 * 2**20),
        cost_estimate=pl.CostEstimate(
            flops=FACTOR_FLOPS, bytes_accessed=9 * 2**20, transcendentals=0
        ),
        name="factor_pivots",
    )(row_index.astype(jnp.int32).reshape(1), parts)


def finish_kernel(
    meta_ref,
    front_ref,
    child_ref,
    received_ref,
    across_refs,
    beneath_ref,
    upper_ref,
    inverse_ref,
    out_ref,
    upper_parts_ref,
    wide_parts_ref,
    across_ref,
    solved_ref,
    solved_parts_ref,
):
    half_step = pl.program_id(0)
    sibling = meta_ref[0]
    row_index = meta_ref[1]
    column_index = meta_ref[2]
    width = across_ref.shape[1]
    column_rows = slice(2 * width, 3 * width)

    def solve(count, source):
        for j in range(PIVOT_TILES // 2):
            columns = slice(2 * j * TILE, 2 * (j + 1) * TILE)
            rest = jnp.concatenate([source(2 * j), source(2 * j + 1)], axis=1)
            if j:
                before = slice(0, 2 * j * TILE)
                rest = rest - parts_dot(
                    [ref[:count, before] for ref in solved_parts_ref],
                    [ref[before, columns] for ref in upper_parts_ref],
                    ((1,), (0,)),
                )
            result = parts_dot(split(rest), [ref[j] for ref in wide_parts_ref], ((1,), (0,)))
            solved_ref[:count, columns] = result
            for ref, part in zip(solved_parts_ref, split(result)):
                ref[:count, columns] = part

    def panel(i):
        return [beneath_ref[i, 0], beneath_ref[8 + i, 0]]

    @pl.when(half_step == 0)
    def _():
        for j in range(PIVOT_TILES // 2):
            rows = slice(2 * j * TILE, 2 * (j + 1) * TILE)
            after = slice(2 * (j + 1) * TILE, NPIV)
            if j < PIVOT_TILES // 2 - 1:
                for ref, part in zip(upper_parts_ref, split(upper_ref[rows, after])):
                    ref[rows, after] = part
            low, high = inverse_ref[2 * j], inverse_ref[2 * j + 1]
            between = upper_ref[
                2 * j * TILE : (2 * j + 1) * TILE, (2 * j + 1) * TILE : 2 * (j + 1) * TILE
            ]
            corner = -exact_dot(low, exact_dot(between, high))
            for ref, l, h, c in zip(wide_parts_ref, split(low), split(high), split(corner)):
                ref[j, :TILE, :TILE] = l
                ref[j, TILE:, TILE:] = h
                ref[j, :TILE, TILE:] = c
                ref[j, TILE:, :TILE] = jnp.zeros((TILE, TILE), jnp.bfloat16)

        for behind, ref in zip(RING, across_refs):
            across_ref[lax.rem(row_index - behind + 8, 8)] = ref[...]
        solve(3 * width, lambda i: jnp.concatenate(panel(i) + [across_ref[i]]))

    @pl.when(half_step > 0)
    def _():
        solve(2 * width, lambda i: jnp.concatenate(panel(i)))

    update = parts_dot(
        [ref[: 2 * width] for ref in solved_parts_ref],
        [ref[column_rows] for ref in solved_parts_ref],
        ((1,), (1,)),
    )

    for half in range(2):
        group = 2 * half_step + half

        def row_slot(s, u):
            return meta_ref[4 + s * 8 + group * 2 + u]

        def column_slot(s, u):
            return meta_ref[20 + s * 2 + u]

        for m in range(3):
            for n in range(3):
                lanes = slice(n * TILE, (n + 1) * TILE)
                total = front_ref[m, half, :, lanes]
                for u in range(2):
                    for v in range(2):
                        if m - u in (0, 1) and n - v in (0, 1):
                            own = (row_slot(sibling, u) == m) & (column_slot(sibling, v) == n)
                            other = (row_slot(1 - sibling, u) == m) & (
                                column_slot(1 - sibling, v) == n
                            )
                            own_lanes = pl.ds(
                                pl.multiple_of((2 * v + sibling) * TILE, TILE), TILE
                            )
                            mine = child_ref[u, half, :, own_lanes]
                            theirs = received_ref[v, u, half]
                            total = total + jnp.where(own, mine, 0.0)
                            total = total + jnp.where(other, theirs, 0.0)
                top = half * width + m * TILE
                out_ref[m, half, :, lanes] = (
                    total - update[top : top + TILE, n * TILE : (n + 1) * TILE]
                )

    pivot_column = column_index < PIVOT_TILES
    own_column = pl.ds(pl.multiple_of(lax.rem(column_index, 8) * TILE, TILE), TILE)

    @pl.when(pivot_column)
    def _():
        for half in range(2):
            for m in range(3):
                top = half * width + m * TILE
                out_ref[m, half, :, :TILE] = solved_ref[top : top + TILE, own_column]

    @pl.when(half_step == 0)
    def _():
        own_row = pl.ds(pl.multiple_of(row_index * TILE, TILE), TILE)
        for n in range(3):
            lanes = slice(n * TILE, (n + 1) * TILE)
            top = 2 * width + n * TILE
            out_ref[0, 0, :, lanes] = solved_ref[top : top + TILE, own_row].T

        @pl.when(pivot_column)
        def _():
            @pl.when(row_index < column_index)
            def _():
                out_ref[0, 0, :, :TILE] = upper_ref[own_row, own_column]

            @pl.when(row_index > column_index)
            def _():
                out_ref[0, 0, :, :TILE] = upper_ref[own_column, own_row].T

            @pl.when(row_index == column_index)
            def _():
                row = lax.broadcasted_iota(jnp.int32, (TILE, TILE), 0)
                lane = lax.broadcasted_iota(jnp.int32, (TILE, TILE), 1)
                tile = upper_ref[own_row, own_column]
                out_ref[0, 0, :, :TILE] = jnp.where(row > lane, tile.T, tile)


def finish(meta, front, child, received, across, beneath, upper, inverse):
    width = front.shape[1]
    whole = pl.BlockSpec(memory_space=pltpu.VMEM)
    held = lambda *shape: [pltpu.VMEM(shape, jnp.bfloat16) for _ in range(PARTS)]
    out = pl.pallas_call(
        finish_kernel,
        grid=(2,),
        out_shape=jax.ShapeDtypeStruct((3, 4, TILE, width), jnp.float32),
        in_specs=[
            pl.BlockSpec(memory_space=pltpu.SMEM),
            pl.BlockSpec((3, 2, TILE, width), lambda g: (0, g, 0, 0)),
            pl.BlockSpec((2, 2, TILE, 4 * TILE), lambda g: (0, g, 0, 0)),
            pl.BlockSpec((2, 2, 2, TILE, TILE), lambda g: (0, 0, g, 0, 0)),
            [whole] * 8,
            pl.BlockSpec((16, 1, width, TILE), lambda g: (0, g, 0, 0)),
            whole,
            whole,
        ],
        out_specs=pl.BlockSpec((3, 2, TILE, width), lambda g: (0, g, 0, 0)),
        scratch_shapes=[
            held(NPIV, NPIV),
            held(PIVOT_TILES // 2, 2 * TILE, 2 * TILE),
            pltpu.VMEM((8, width, TILE), jnp.float32),
            pltpu.VMEM((3 * width, NPIV), jnp.float32),
            held(3 * width, NPIV),
        ],
        compiler_params=pltpu.CompilerParams(vmem_limit_bytes=50 * 2**20),
        cost_estimate=pl.CostEstimate(
            flops=15 * 10**9, bytes_accessed=24 * 2**20, transcendentals=0
        ),
        name="solve_and_update",
    )(
        meta,
        front.reshape(3, 4, TILE, width),
        child.reshape(2, 4, TILE, 4 * TILE),
        received.reshape(2, 2, 4, TILE, TILE),
        across,
        beneath,
        upper,
        inverse,
    )
    return out.reshape(front.shape)


ALL = ("pair", "row", "col")
SWAP = [(0, 1), (1, 0)]
RING = (0, 1, 7, 2, 6, 3, 5, 4)


def at(pair, row, col):
    return (pair * 8 + row) * 16 + col


def ring_gather(block, beside):
    up = [(i, (i + 1) % 8) for i in range(8)]
    down = [(i, (i - 1) % 8) for i in range(8)]
    half = block.shape[0] // 2
    behind = ahead = block
    blocks = [block]
    for turn in range(3):
        behind = lax.ppermute(behind, "row", up)
        ahead = lax.ppermute(ahead, "row", down)
        if turn:
            behind, ahead, beside[turn - 1] = lax.optimization_barrier(
                (behind, ahead, beside[turn - 1])
            )
        blocks += [behind, ahead]
    last = [lax.ppermute(behind[:half], "row", up), lax.ppermute(ahead[half:], "row", down)]
    return blocks + [jnp.concatenate(last)]


def assemble_kernel(meta_ref, front_ref, child_ref, came_ref, out_ref):
    sibling = meta_ref[0]
    own_row = meta_ref[4 + sibling * 8] == 0
    other_row = meta_ref[4 + (1 - sibling) * 8] == 0
    for n in range(3):
        total = front_ref[:, n * TILE : (n + 1) * TILE]
        for v in range(2):
            if n - v in (0, 1):
                own = own_row & (meta_ref[20 + sibling * 2 + v] == n)
                other = other_row & (meta_ref[20 + (1 - sibling) * 2 + v] == n)
                lanes = pl.ds(pl.multiple_of((2 * v + sibling) * TILE, TILE), TILE)
                total = total + jnp.where(own, child_ref[:, lanes], 0.0)
                total = total + jnp.where(other, came_ref[v], 0.0)
        out_ref[n * TILE : (n + 1) * TILE, :] = total.T


def assemble(meta, front, child, came):
    width = front.shape[1]
    return pl.pallas_call(
        assemble_kernel,
        grid=(1,),
        out_shape=jax.ShapeDtypeStruct((width, TILE), jnp.float32),
        in_specs=[
            pl.BlockSpec(memory_space=pltpu.SMEM),
            pl.BlockSpec((TILE, width), lambda g: (0, 0)),
            pl.BlockSpec((TILE, 4 * TILE), lambda g: (0, 0)),
            pl.BlockSpec((2, TILE, TILE), lambda g: (0, 0, 0)),
        ],
        out_specs=pl.BlockSpec((width, TILE), lambda g: (0, 0)),
        compiler_params=pltpu.CompilerParams(vmem_limit_bytes=8 * 2**20),
        name="assemble_pivot_rows",
    )(meta, front, child, came)


def body(front_init, child_blocks, tile_map):
    sibling = lax.axis_index("pair")
    row_index = lax.axis_index("row")
    col_index = lax.axis_index("col")
    half_index = col_index // 8
    column_index = sibling * 16 + col_index
    own = child_blocks[0]
    positions = tile_map.astype(jnp.int32).reshape(2, 2, 32) // 32

    def pick(count, v, even):
        low = own[:count, 2 * v * TILE : (2 * v + 1) * TILE]
        high = own[:count, (2 * v + 1) * TILE : 2 * (v + 1) * TILE]
        return jnp.where(even, low, high)

    with jax.named_scope("pivot_block"):
        own_positions = positions[sibling, 0]
        hit = (own_positions[row_index] == 0) & (own_positions[col_index] == 0)
        tile = jnp.where(sibling == 0, front_init[:TILE, :TILE], 0.0)
        tile = tile + jnp.where(hit, own[:TILE, :TILE], 0.0)
        upper_half, lower_half = tile[: TILE // 2], tile[TILE // 2 :]
        mine = jnp.where(half_index == 0, upper_half, 0.0)
        places = [(p, i, c) for p in range(2) for i in range(8) for c in range(8)]
        mine = (
            mine
            + lax.ppermute(upper_half, ALL, [(at(p, i, c), at(1 - p, i, c)) for p, i, c in places])
            + lax.ppermute(lower_half, ALL, [(at(p, i, c), at(p, i, c + 8)) for p, i, c in places])
            + lax.ppermute(
                lower_half, ALL, [(at(p, i, c), at(1 - p, i, c + 8)) for p, i, c in places]
            )
        )
    with jax.named_scope("siblings"):
        handed = jnp.stack([pick(NPIV, v, sibling != 0) for v in range(2)])
        handed, mine = lax.optimization_barrier((handed, mine))
        received = lax.ppermute(handed, "pair", SWAP)

    with jax.named_scope("pivot_gather"):
        mine = mine[None]
        for bit in (4, 2, 1):
            came = lax.ppermute(mine, "row", [(i, i ^ bit) for i in range(8)])
            mine = jnp.concatenate([mine, came])
        mine, received = lax.optimization_barrier((mine, received))
        parts = lax.all_gather(mine, "col")

    row_positions = jnp.swapaxes(
        lax.dynamic_index_in_dim(positions.reshape(2, 2, 4, 8), row_index, 3, keepdims=False), 1, 2
    )
    column_positions = lax.dynamic_index_in_dim(positions, column_index, 2, keepdims=False)
    meta = jnp.concatenate(
        [
            jnp.stack([sibling, row_index, column_index, column_index]),
            row_positions.reshape(16),
            column_positions.reshape(4),
        ]
    ).astype(jnp.int32)

    with jax.named_scope("pivot_rows"):
        pivot_columns = assemble(meta, front_init[:TILE], own[:TILE], received)

    with jax.named_scope("panel"):
        pivot_columns, mine = lax.optimization_barrier((pivot_columns, mine))
        routes = [[], []]
        for p in range(2):
            for i in range(8):
                for c in range(16):
                    half, other = divmod(c, 8)
                    for away in range(2):
                        target = at(p ^ away, other, 8 * half + i)
                        routes[away].append((at(p, i, c), target))
        beside = [lax.ppermute(pivot_columns, ALL, route) for route in routes]
        across = ring_gather(pivot_columns, beside)
        same, crossed = beside
        turned = jnp.where(
            sibling == 0, jnp.stack([same, crossed]), jnp.stack([crossed, same])
        )
        beneath = lax.all_gather(turned, "col")
        across, parts = lax.optimization_barrier((across, parts))

    with jax.named_scope("factor"):
        upper, inverse = factor(row_index, parts)
    with jax.named_scope("finish"):
        return finish(meta, front_init, own, received, across, beneath, upper, inverse)


def solution(mesh):
    return jax.shard_map(
        body,
        mesh=mesh,
        in_specs=(P("row", ("pair", "col")), P("pair", "row", "col"), P()),
        out_specs=P("row", ("pair", "col")),
        check_vma=False,
    )
```

```python
import jax
import jax.numpy as jnp
from jax import lax
from jax.experimental import pallas as pl
from jax.experimental.pallas import tpu as pltpu
from jax.sharding import PartitionSpec as P

TILE = 128
PIVOT_TILES = 8
NPIV = TILE * PIVOT_TILES
STRIP = 64
GROUP = 8
PARTS = 2
FACTOR_FLOPS = 50 * 10**9
EXACT = lax.Precision.HIGHEST


def exact_dot(a, b, contract=((1,), (0,))):
    return lax.dot_general(
        a, b, (contract, ((), ())), precision=EXACT, preferred_element_type=jnp.float32
    )


def split(x):
    parts = []
    for _ in range(PARTS):
        part = x.astype(jnp.bfloat16)
        x = x - part.astype(jnp.float32)
        parts.append(part)
    return parts


def parts_dot(a, b, contract):
    pairs = [(i, order - i) for order in range(len(a)) for i in range(order + 1)]
    return lax.dot_general(
        jnp.concatenate([a[i] for i, _ in pairs], axis=contract[0][0]),
        jnp.concatenate([b[j] for _, j in pairs], axis=contract[1][0]),
        (contract, ((), ())),
        preferred_element_type=jnp.float32,
    )


def factor_tile(block):
    row = lax.broadcasted_iota(jnp.int32, (TILE, TILE), 0)
    lane = lax.broadcasted_iota(jnp.int32, (TILE, TILE), 1)
    remaining = jnp.concatenate([block, (row == lane).astype(jnp.float32)], axis=1)
    group_row = lax.broadcasted_iota(jnp.int32, (GROUP, 2 * TILE), 0)

    def twice(x):
        return jnp.concatenate([x, x], axis=1)

    def tall(x, count):
        return jnp.concatenate([x] * (count // GROUP), axis=0)

    done = []
    for first in range(0, TILE, STRIP):
        strip = remaining[:STRIP]
        finished = []
        for k in range(0, STRIP, GROUP):
            at = first + k
            count = STRIP - k - GROUP
            top, beneath = strip[:GROUP], strip[GROUP:]
            columns, rows, corner, inverse = [], [], {}, []
            for t in range(GROUP):
                if count:
                    columns.append(jnp.broadcast_to(beneath[:, at + t : at + t + 1], (count, TILE)))
                rows.append(jnp.broadcast_to(top[t : t + 1], (GROUP, 2 * TILE)))
                for r in range(t + 1):
                    corner[r, t] = jnp.broadcast_to(
                        top[r : r + 1, at + t : at + t + 1], (GROUP, TILE)
                    )
            for r in range(GROUP):
                inverse.append(1.0 / corner[r, r])
                for t in range(r + 1, GROUP):
                    scale = corner[r, t] * inverse[r]
                    for u in range(t, GROUP):
                        product = corner[r, t] * corner[r, u]
                        corner[t, u] = corner[t, u] - product * inverse[r]
                    if count:
                        columns[t] = columns[t] - tall(scale, count) * columns[r]
                    rows[t] = rows[t] - twice(scale) * rows[r]
            if count:
                for t in range(GROUP):
                    share = columns[t] * tall(inverse[t], count)
                    beneath = beneath - twice(share) * tall(rows[t], count)
            result = None
            for t in range(GROUP):
                root = lax.rsqrt(corner[t, t])
                root = root * (1.5 - 0.5 * corner[t, t] * root * root)
                scaled = rows[t] * twice(root)
                result = scaled if t == 0 else jnp.where(group_row == t, scaled, result)
            finished.append(result)
            strip = beneath
        strip = jnp.concatenate(finished, axis=0)
        done.append(strip)
        if first + STRIP < TILE:
            change = exact_dot(strip[:, :TILE], strip, ((0,), (0,)))
            remaining = remaining[STRIP:] - change[first + STRIP :]
    whole = jnp.concatenate(done, axis=0)
    return jnp.where(lane >= row, whole[:, :TILE], 0.0), whole[:, TILE:]


def solve(source, upper_parts_ref, wide_parts_ref, solved_ref, solved_parts_ref):
    for j in range(PIVOT_TILES // 2):
        columns = slice(2 * j * TILE, 2 * (j + 1) * TILE)
        rest = jnp.concatenate([source(2 * j), source(2 * j + 1)], axis=1)
        if j:
            before = slice(0, 2 * j * TILE)
            rest = rest - parts_dot(
                [ref[:, before] for ref in solved_parts_ref],
                [ref[before, columns] for ref in upper_parts_ref],
                ((1,), (0,)),
            )
        result = parts_dot(split(rest), [ref[j] for ref in wide_parts_ref], ((1,), (0,)))
        solved_ref[:, columns] = result
        for ref, part in zip(solved_parts_ref, split(result)):
            ref[:, columns] = part


def factor_kernel(
    meta_ref,
    parts_ref,
    across_refs,
    upper_parts_ref,
    wide_parts_ref,
    column_parts_ref,
    pivot_ref,
    upper_ref,
    inverse_ref,
    across_ref,
    solved_ref,
):
    row_index = meta_ref[1]
    column_index = meta_ref[2]
    for i in range(PIVOT_TILES):
        away = i ^ row_index
        place = (away & 1) * 4 + (away & 2) + (away >> 2)
        for c in range(i, PIVOT_TILES):
            for half in range(2):
                upper_ref[pl.ds(i * TILE + half * 64, 64), pl.ds(c * TILE, TILE)] = parts_ref[
                    half * 8 + c, place
                ]

    def step(j, carry):
        at = pl.ds(pl.multiple_of(j * TILE, TILE), TILE)
        upper, inverse = factor_tile(upper_ref[at, at])
        upper_ref[at, at] = upper
        inverse_ref[j] = inverse.T
        for now in range(PIVOT_TILES - 1):

            @pl.when(j == now)
            def _():
                here = slice(now * TILE, (now + 1) * TILE)
                after = slice((now + 1) * TILE, NPIV)
                solved = parts_dot(split(inverse), split(upper_ref[here, after]), ((1,), (0,)))
                upper_ref[here, after] = solved
                solved_parts = split(solved)
                for k in range(now + 1, PIVOT_TILES):
                    rows = slice(k * TILE, (k + 1) * TILE)
                    rest = slice(k * TILE, NPIV)
                    offset = (k - now - 1) * TILE
                    upper_ref[rows, rest] = upper_ref[rows, rest] - parts_dot(
                        [part[:, offset : offset + TILE] for part in solved_parts],
                        [part[:, offset:] for part in solved_parts],
                        ((0,), (0,)),
                    )

        return carry

    lax.fori_loop(0, PIVOT_TILES, step, 0)

    for j in range(PIVOT_TILES // 2):
        rows = slice(2 * j * TILE, 2 * (j + 1) * TILE)
        after = slice(2 * (j + 1) * TILE, NPIV)
        if j < PIVOT_TILES // 2 - 1:
            for ref, part in zip(upper_parts_ref, split(upper_ref[rows, after])):
                ref[rows, after] = part
        low, high = inverse_ref[2 * j], inverse_ref[2 * j + 1]
        between = upper_ref[
            2 * j * TILE : (2 * j + 1) * TILE, (2 * j + 1) * TILE : 2 * (j + 1) * TILE
        ]
        corner = -exact_dot(low, exact_dot(between, high))
        for ref, l, h, c in zip(wide_parts_ref, split(low), split(high), split(corner)):
            ref[j, :TILE, :TILE] = l
            ref[j, TILE:, TILE:] = h
            ref[j, :TILE, TILE:] = c
            ref[j, TILE:, :TILE] = jnp.zeros((TILE, TILE), jnp.bfloat16)

    for behind, ref in zip(RING, across_refs):
        across_ref[lax.rem(row_index - behind + 8, 8)] = ref[...]
    solve(
        lambda i: across_ref[i], upper_parts_ref, wide_parts_ref, solved_ref, column_parts_ref
    )

    own_row = pl.ds(pl.multiple_of(row_index * TILE, TILE), TILE)
    own_column = pl.ds(pl.multiple_of(lax.rem(column_index, 8) * TILE, TILE), TILE)
    for n in range(3):
        lanes = slice(n * TILE, (n + 1) * TILE)
        pivot_ref[:, lanes] = solved_ref[lanes, own_row].T

    @pl.when(column_index < PIVOT_TILES)
    def _():
        @pl.when(row_index < column_index)
        def _():
            pivot_ref[:, :TILE] = upper_ref[own_row, own_column]

        @pl.when(row_index > column_index)
        def _():
            pivot_ref[:, :TILE] = upper_ref[own_column, own_row].T

        @pl.when(row_index == column_index)
        def _():
            row = lax.broadcasted_iota(jnp.int32, (TILE, TILE), 0)
            lane = lax.broadcasted_iota(jnp.int32, (TILE, TILE), 1)
            tile = upper_ref[own_row, own_column]
            pivot_ref[:, :TILE] = jnp.where(row > lane, tile.T, tile)


def factor(meta, parts, across):
    width = across[0].shape[0]
    whole = pl.BlockSpec(memory_space=pltpu.VMEM)
    halves = lambda *shape: [jax.ShapeDtypeStruct(shape, jnp.bfloat16) for _ in range(PARTS)]
    return pl.pallas_call(
        factor_kernel,
        out_shape=(
            halves(NPIV, NPIV),
            halves(PIVOT_TILES // 2, 2 * TILE, 2 * TILE),
            halves(width, NPIV),
            jax.ShapeDtypeStruct((TILE, width), jnp.float32),
        ),
        in_specs=[pl.BlockSpec(memory_space=pltpu.SMEM), whole, [whole] * 8],
        out_specs=([whole] * PARTS, [whole] * PARTS, [whole] * PARTS, whole),
        scratch_shapes=[
            pltpu.VMEM((NPIV, NPIV), jnp.float32),
            pltpu.VMEM((PIVOT_TILES, TILE, TILE), jnp.float32),
            pltpu.VMEM((8, width, TILE), jnp.float32),
            pltpu.VMEM((width, NPIV), jnp.float32),
        ],
        compiler_params=pltpu.CompilerParams(vmem_limit_bytes=36 * 2**20),
        cost_estimate=pl.CostEstimate(
            flops=FACTOR_FLOPS, bytes_accessed=9 * 2**20, transcendentals=0
        ),
        name="factor_pivots",
    )(meta, parts, across)


def finish_kernel(
    meta_ref,
    front_ref,
    child_ref,
    received_ref,
    beneath_ref,
    upper_parts_ref,
    wide_parts_ref,
    column_parts_ref,
    pivot_ref,
    out_ref,
    solved_ref,
    solved_parts_ref,
):
    half_step = pl.program_id(0)
    sibling = meta_ref[0]
    column_index = meta_ref[2]
    width = pivot_ref.shape[1]

    solve(
        lambda i: jnp.concatenate([beneath_ref[i, 0], beneath_ref[8 + i, 0]]),
        upper_parts_ref,
        wide_parts_ref,
        solved_ref,
        solved_parts_ref,
    )
    update = parts_dot(
        [ref[...] for ref in solved_parts_ref],
        [ref[...] for ref in column_parts_ref],
        ((1,), (1,)),
    )

    for half in range(2):
        group = 2 * half_step + half

        def row_slot(s, u):
            return meta_ref[4 + s * 8 + group * 2 + u]

        def column_slot(s, u):
            return meta_ref[20 + s * 2 + u]

        for m in range(3):
            for n in range(3):
                lanes = slice(n * TILE, (n + 1) * TILE)
                total = front_ref[m, half, :, lanes]
                for u in range(2):
                    for v in range(2):
                        if m - u in (0, 1) and n - v in (0, 1):
                            own = (row_slot(sibling, u) == m) & (column_slot(sibling, v) == n)
                            other = (row_slot(1 - sibling, u) == m) & (
                                column_slot(1 - sibling, v) == n
                            )
                            own_lanes = pl.ds(
                                pl.multiple_of((2 * v + sibling) * TILE, TILE), TILE
                            )
                            mine = child_ref[u, half, :, own_lanes]
                            theirs = received_ref[v, u, half]
                            total = total + jnp.where(own, mine, 0.0)
                            total = total + jnp.where(other, theirs, 0.0)
                top = half * width + m * TILE
                out_ref[m, half, :, lanes] = (
                    total - update[top : top + TILE, n * TILE : (n + 1) * TILE]
                )

    pivot_column = column_index < PIVOT_TILES
    own_column = pl.ds(pl.multiple_of(lax.rem(column_index, 8) * TILE, TILE), TILE)

    @pl.when(pivot_column)
    def _():
        for half in range(2):
            for m in range(3):
                top = half * width + m * TILE
                out_ref[m, half, :, :TILE] = solved_ref[top : top + TILE, own_column]

    @pl.when(half_step == 0)
    def _():
        out_ref[0, 0, :, :] = pivot_ref[...]


def finish(meta, front, child, received, beneath, upper, wide, column, pivot):
    width = front.shape[1]
    whole = pl.BlockSpec(memory_space=pltpu.VMEM)
    held = lambda *shape: [pltpu.VMEM(shape, jnp.bfloat16) for _ in range(PARTS)]
    out = pl.pallas_call(
        finish_kernel,
        grid=(2,),
        out_shape=jax.ShapeDtypeStruct((3, 4, TILE, width), jnp.float32),
        in_specs=[
            pl.BlockSpec(memory_space=pltpu.SMEM),
            pl.BlockSpec((3, 2, TILE, width), lambda g: (0, g, 0, 0)),
            pl.BlockSpec((2, 2, TILE, 4 * TILE), lambda g: (0, g, 0, 0)),
            pl.BlockSpec((2, 2, 2, TILE, TILE), lambda g: (0, 0, g, 0, 0)),
            pl.BlockSpec((16, 1, width, TILE), lambda g: (0, g, 0, 0)),
            [whole] * PARTS,
            [whole] * PARTS,
            [whole] * PARTS,
            whole,
        ],
        out_specs=pl.BlockSpec((3, 2, TILE, width), lambda g: (0, g, 0, 0)),
        scratch_shapes=[
            pltpu.VMEM((2 * width, NPIV), jnp.float32),
            held(2 * width, NPIV),
        ],
        compiler_params=pltpu.CompilerParams(vmem_limit_bytes=50 * 2**20),
        cost_estimate=pl.CostEstimate(
            flops=15 * 10**9, bytes_accessed=24 * 2**20, transcendentals=0
        ),
        name="solve_and_update",
    )(
        meta,
        front.reshape(3, 4, TILE, width),
        child.reshape(2, 4, TILE, 4 * TILE),
        received.reshape(2, 2, 4, TILE, TILE),
        beneath,
        upper,
        wide,
        column,
        pivot,
    )
    return out.reshape(front.shape)


ALL = ("pair", "row", "col")
SWAP = [(0, 1), (1, 0)]
RING = (0, 1, 7, 2, 6, 3, 5, 4)


def at(pair, row, col):
    return (pair * 8 + row) * 16 + col


def ring_gather(block, beside):
    up = [(i, (i + 1) % 8) for i in range(8)]
    down = [(i, (i - 1) % 8) for i in range(8)]
    half = block.shape[0] // 2
    behind = ahead = block
    blocks = [block]
    for turn in range(3):
        behind = lax.ppermute(behind, "row", up)
        ahead = lax.ppermute(ahead, "row", down)
        if turn:
            behind, ahead, beside[turn - 1] = lax.optimization_barrier(
                (behind, ahead, beside[turn - 1])
            )
        blocks += [behind, ahead]
    last = [lax.ppermute(behind[:half], "row", up), lax.ppermute(ahead[half:], "row", down)]
    return blocks + [jnp.concatenate(last)]


def assemble_kernel(meta_ref, front_ref, child_ref, came_ref, out_ref):
    sibling = meta_ref[0]
    own_row = meta_ref[4 + sibling * 8] == 0
    other_row = meta_ref[4 + (1 - sibling) * 8] == 0
    for n in range(3):
        total = front_ref[:, n * TILE : (n + 1) * TILE]
        for v in range(2):
            if n - v in (0, 1):
                own = own_row & (meta_ref[20 + sibling * 2 + v] == n)
                other = other_row & (meta_ref[20 + (1 - sibling) * 2 + v] == n)
                lanes = pl.ds(pl.multiple_of((2 * v + sibling) * TILE, TILE), TILE)
                total = total + jnp.where(own, child_ref[:, lanes], 0.0)
                total = total + jnp.where(other, came_ref[v], 0.0)
        out_ref[n * TILE : (n + 1) * TILE, :] = total.T


def assemble(meta, front, child, came):
    width = front.shape[1]
    return pl.pallas_call(
        assemble_kernel,
        grid=(1,),
        out_shape=jax.ShapeDtypeStruct((width, TILE), jnp.float32),
        in_specs=[
            pl.BlockSpec(memory_space=pltpu.SMEM),
            pl.BlockSpec((TILE, width), lambda g: (0, 0)),
            pl.BlockSpec((TILE, 4 * TILE), lambda g: (0, 0)),
            pl.BlockSpec((2, TILE, TILE), lambda g: (0, 0, 0)),
        ],
        out_specs=pl.BlockSpec((width, TILE), lambda g: (0, 0)),
        compiler_params=pltpu.CompilerParams(vmem_limit_bytes=8 * 2**20),
        name="assemble_pivot_rows",
    )(meta, front, child, came)


def body(front_init, child_blocks, tile_map):
    sibling = lax.axis_index("pair")
    row_index = lax.axis_index("row")
    col_index = lax.axis_index("col")
    half_index = col_index // 8
    column_index = sibling * 16 + col_index
    own = child_blocks[0]
    positions = tile_map.astype(jnp.int32).reshape(2, 2, 32) // 32

    def pick(count, v, even):
        low = own[:count, 2 * v * TILE : (2 * v + 1) * TILE]
        high = own[:count, (2 * v + 1) * TILE : 2 * (v + 1) * TILE]
        return jnp.where(even, low, high)

    with jax.named_scope("pivot_block"):
        own_positions = positions[sibling, 0]
        hit = (own_positions[row_index] == 0) & (own_positions[col_index] == 0)
        tile = jnp.where(sibling == 0, front_init[:TILE, :TILE], 0.0)
        tile = tile + jnp.where(hit, own[:TILE, :TILE], 0.0)
        upper_half, lower_half = tile[: TILE // 2], tile[TILE // 2 :]
        mine = jnp.where(half_index == 0, upper_half, 0.0)
        places = [(p, i, c) for p in range(2) for i in range(8) for c in range(8)]
        mine = (
            mine
            + lax.ppermute(upper_half, ALL, [(at(p, i, c), at(1 - p, i, c)) for p, i, c in places])
            + lax.ppermute(lower_half, ALL, [(at(p, i, c), at(p, i, c + 8)) for p, i, c in places])
            + lax.ppermute(
                lower_half, ALL, [(at(p, i, c), at(1 - p, i, c + 8)) for p, i, c in places]
            )
        )
    with jax.named_scope("siblings"):
        handed = jnp.stack([pick(NPIV, v, sibling != 0) for v in range(2)])
        handed, mine = lax.optimization_barrier((handed, mine))
        received = lax.ppermute(handed, "pair", SWAP)

    with jax.named_scope("pivot_gather"):
        mine = mine[None]
        for bit in (4, 2, 1):
            came = lax.ppermute(mine, "row", [(i, i ^ bit) for i in range(8)])
            mine = jnp.concatenate([mine, came])
        mine, received = lax.optimization_barrier((mine, received))
        parts = lax.all_gather(mine, "col")

    row_positions = jnp.swapaxes(
        lax.dynamic_index_in_dim(positions.reshape(2, 2, 4, 8), row_index, 3, keepdims=False), 1, 2
    )
    column_positions = lax.dynamic_index_in_dim(positions, column_index, 2, keepdims=False)
    meta = jnp.concatenate(
        [
            jnp.stack([sibling, row_index, column_index, column_index]),
            row_positions.reshape(16),
            column_positions.reshape(4),
        ]
    ).astype(jnp.int32)

    with jax.named_scope("pivot_rows"):
        pivot_columns = assemble(meta, front_init[:TILE], own[:TILE], received)

    with jax.named_scope("panel"):
        pivot_columns, mine = lax.optimization_barrier((pivot_columns, mine))
        routes = [[], []]
        for p in range(2):
            for i in range(8):
                for c in range(16):
                    half, other = divmod(c, 8)
                    for away in range(2):
                        target = at(p ^ away, other, 8 * half + i)
                        routes[away].append((at(p, i, c), target))
        beside = [lax.ppermute(pivot_columns, ALL, route) for route in routes]
        across = ring_gather(pivot_columns, beside)
        same, crossed = beside
        turned = jnp.where(
            sibling == 0, jnp.stack([same, crossed]), jnp.stack([crossed, same])
        )
        beneath = lax.all_gather(turned, "col")
        across, parts = lax.optimization_barrier((across, parts))

    with jax.named_scope("factor"):
        factors = factor(meta, parts, across)
    with jax.named_scope("finish"):
        return finish(meta, front_init, own, received, beneath, *factors)


def solution(mesh):
    return jax.shard_map(
        body,
        mesh=mesh,
        in_specs=(P("row", ("pair", "col")), P("pair", "row", "col"), P()),
        out_specs=P("row", ("pair", "col")),
        check_vma=False,
    )
```

```python
import jax
import jax.numpy as jnp
from jax import lax
from jax.experimental import pallas as pl
from jax.experimental.pallas import tpu as pltpu
from jax.sharding import PartitionSpec as P

TILE = 128
PIVOT_TILES = 8
NPIV = TILE * PIVOT_TILES
STRIP = 64
GROUP = 8
PARTS = 2
FACTOR_FLOPS = 50 * 10**9
EXACT = lax.Precision.HIGHEST


def exact_dot(a, b, contract=((1,), (0,))):
    return lax.dot_general(
        a, b, (contract, ((), ())), precision=EXACT, preferred_element_type=jnp.float32
    )


def split(x):
    parts = []
    for _ in range(PARTS):
        part = x.astype(jnp.bfloat16)
        x = x - part.astype(jnp.float32)
        parts.append(part)
    return parts


def parts_dot(a, b, contract):
    pairs = [(i, order - i) for order in range(len(a)) for i in range(order + 1)]
    return lax.dot_general(
        jnp.concatenate([a[i] for i, _ in pairs], axis=contract[0][0]),
        jnp.concatenate([b[j] for _, j in pairs], axis=contract[1][0]),
        (contract, ((), ())),
        preferred_element_type=jnp.float32,
    )


def factor_tile(block):
    row = lax.broadcasted_iota(jnp.int32, (TILE, TILE), 0)
    lane = lax.broadcasted_iota(jnp.int32, (TILE, TILE), 1)
    remaining = jnp.concatenate([block, (row == lane).astype(jnp.float32)], axis=1)
    group_row = lax.broadcasted_iota(jnp.int32, (GROUP, 2 * TILE), 0)

    def twice(x):
        return jnp.concatenate([x, x], axis=1)

    def tall(x, count):
        return jnp.concatenate([x] * (count // GROUP), axis=0)

    done = []
    for first in range(0, TILE, STRIP):
        strip = remaining[:STRIP]
        finished = []
        for k in range(0, STRIP, GROUP):
            at = first + k
            count = STRIP - k - GROUP
            top, beneath = strip[:GROUP], strip[GROUP:]
            columns, rows, corner, inverse = [], [], {}, []
            for t in range(GROUP):
                if count:
                    columns.append(jnp.broadcast_to(beneath[:, at + t : at + t + 1], (count, TILE)))
                rows.append(jnp.broadcast_to(top[t : t + 1], (GROUP, 2 * TILE)))
                for r in range(t + 1):
                    corner[r, t] = jnp.broadcast_to(
                        top[r : r + 1, at + t : at + t + 1], (GROUP, TILE)
                    )
            for r in range(GROUP):
                inverse.append(1.0 / corner[r, r])
                for t in range(r + 1, GROUP):
                    scale = corner[r, t] * inverse[r]
                    for u in range(t, GROUP):
                        product = corner[r, t] * corner[r, u]
                        corner[t, u] = corner[t, u] - product * inverse[r]
                    if count:
                        columns[t] = columns[t] - tall(scale, count) * columns[r]
                    rows[t] = rows[t] - twice(scale) * rows[r]
            if count:
                for t in range(GROUP):
                    share = columns[t] * tall(inverse[t], count)
                    beneath = beneath - twice(share) * tall(rows[t], count)
            result = None
            for t in range(GROUP):
                root = lax.rsqrt(corner[t, t])
                root = root * (1.5 - 0.5 * corner[t, t] * root * root)
                scaled = rows[t] * twice(root)
                result = scaled if t == 0 else jnp.where(group_row == t, scaled, result)
            finished.append(result)
            strip = beneath
        strip = jnp.concatenate(finished, axis=0)
        done.append(strip)
        if first + STRIP < TILE:
            change = exact_dot(strip[:, :TILE], strip, ((0,), (0,)))
            remaining = remaining[STRIP:] - change[first + STRIP :]
    whole = jnp.concatenate(done, axis=0)
    return jnp.where(lane >= row, whole[:, :TILE], 0.0), whole[:, TILE:]


def solve(source, upper_parts_ref, wide_parts_ref, solved_ref, solved_parts_ref):
    for j in range(PIVOT_TILES // 2):
        columns = slice(2 * j * TILE, 2 * (j + 1) * TILE)
        rest = jnp.concatenate([source(2 * j), source(2 * j + 1)], axis=1)
        if j:
            before = slice(0, 2 * j * TILE)
            rest = rest - parts_dot(
                [ref[:, before] for ref in solved_parts_ref],
                [ref[before, columns] for ref in upper_parts_ref],
                ((1,), (0,)),
            )
        result = parts_dot(split(rest), [ref[j] for ref in wide_parts_ref], ((1,), (0,)))
        solved_ref[:, columns] = result
        for ref, part in zip(solved_parts_ref, split(result)):
            ref[:, columns] = part


def factor_kernel(
    meta_ref,
    parts_ref,
    across_refs,
    upper_parts_ref,
    wide_parts_ref,
    column_parts_ref,
    pivot_ref,
    upper_ref,
    inverse_ref,
    across_ref,
    solved_ref,
):
    row_index = meta_ref[1]
    column_index = meta_ref[2]
    for i in range(PIVOT_TILES):
        away = i ^ row_index
        place = (away & 1) * 4 + (away & 2) + (away >> 2)
        for c in range(i, PIVOT_TILES):
            for half in range(2):
                upper_ref[pl.ds(i * TILE + half * 64, 64), pl.ds(c * TILE, TILE)] = parts_ref[
                    half * 8 + c, place
                ]

    def step(j, carry):
        at = pl.ds(pl.multiple_of(j * TILE, TILE), TILE)
        upper, inverse = factor_tile(upper_ref[at, at])
        upper_ref[at, at] = upper
        inverse_ref[j] = inverse.T
        for now in range(PIVOT_TILES - 1):

            @pl.when(j == now)
            def _():
                here = slice(now * TILE, (now + 1) * TILE)
                after = slice((now + 1) * TILE, NPIV)
                solved = parts_dot(split(inverse), split(upper_ref[here, after]), ((1,), (0,)))
                upper_ref[here, after] = solved
                solved_parts = split(solved)
                for k in range(now + 1, PIVOT_TILES):
                    rows = slice(k * TILE, (k + 1) * TILE)
                    rest = slice(k * TILE, NPIV)
                    offset = (k - now - 1) * TILE
                    upper_ref[rows, rest] = upper_ref[rows, rest] - parts_dot(
                        [part[:, offset : offset + TILE] for part in solved_parts],
                        [part[:, offset:] for part in solved_parts],
                        ((0,), (0,)),
                    )

        return carry

    lax.fori_loop(0, PIVOT_TILES, step, 0)

    for j in range(PIVOT_TILES // 2):
        rows = slice(2 * j * TILE, 2 * (j + 1) * TILE)
        after = slice(2 * (j + 1) * TILE, NPIV)
        if j < PIVOT_TILES // 2 - 1:
            for ref, part in zip(upper_parts_ref, split(upper_ref[rows, after])):
                ref[rows, after] = part
        low, high = inverse_ref[2 * j], inverse_ref[2 * j + 1]
        between = upper_ref[
            2 * j * TILE : (2 * j + 1) * TILE, (2 * j + 1) * TILE : 2 * (j + 1) * TILE
        ]
        corner = -exact_dot(low, exact_dot(between, high))
        for ref, l, h, c in zip(wide_parts_ref, split(low), split(high), split(corner)):
            ref[j, :TILE, :TILE] = l
            ref[j, TILE:, TILE:] = h
            ref[j, :TILE, TILE:] = c
            ref[j, TILE:, :TILE] = jnp.zeros((TILE, TILE), jnp.bfloat16)

    for behind, ref in zip(RING, across_refs):
        across_ref[lax.rem(row_index - behind + 8, 8)] = ref[...]
    solve(
        lambda i: across_ref[i], upper_parts_ref, wide_parts_ref, solved_ref, column_parts_ref
    )

    own_row = pl.ds(pl.multiple_of(row_index * TILE, TILE), TILE)
    own_column = pl.ds(pl.multiple_of(lax.rem(column_index, 8) * TILE, TILE), TILE)
    for n in range(3):
        lanes = slice(n * TILE, (n + 1) * TILE)
        pivot_ref[:, lanes] = solved_ref[lanes, own_row].T

    @pl.when(column_index < PIVOT_TILES)
    def _():
        @pl.when(row_index < column_index)
        def _():
            pivot_ref[:, :TILE] = upper_ref[own_row, own_column]

        @pl.when(row_index > column_index)
        def _():
            pivot_ref[:, :TILE] = upper_ref[own_column, own_row].T

        @pl.when(row_index == column_index)
        def _():
            row = lax.broadcasted_iota(jnp.int32, (TILE, TILE), 0)
            lane = lax.broadcasted_iota(jnp.int32, (TILE, TILE), 1)
            tile = upper_ref[own_row, own_column]
            pivot_ref[:, :TILE] = jnp.where(row > lane, tile.T, tile)


def factor(meta, parts, across):
    width = across[0].shape[0]
    whole = pl.BlockSpec(memory_space=pltpu.VMEM)
    halves = lambda *shape: [jax.ShapeDtypeStruct(shape, jnp.bfloat16) for _ in range(PARTS)]
    return pl.pallas_call(
        factor_kernel,
        out_shape=(
            halves(NPIV, NPIV),
            halves(PIVOT_TILES // 2, 2 * TILE, 2 * TILE),
            halves(width, NPIV),
            jax.ShapeDtypeStruct((TILE, width), jnp.float32),
        ),
        in_specs=[pl.BlockSpec(memory_space=pltpu.SMEM), whole, [whole] * 8],
        out_specs=([whole] * PARTS, [whole] * PARTS, [whole] * PARTS, whole),
        scratch_shapes=[
            pltpu.VMEM((NPIV, NPIV), jnp.float32),
            pltpu.VMEM((PIVOT_TILES, TILE, TILE), jnp.float32),
            pltpu.VMEM((8, width, TILE), jnp.float32),
            pltpu.VMEM((width, NPIV), jnp.float32),
        ],
        compiler_params=pltpu.CompilerParams(vmem_limit_bytes=24 * 2**20),
        cost_estimate=pl.CostEstimate(
            flops=FACTOR_FLOPS, bytes_accessed=9 * 2**20, transcendentals=0
        ),
        name="factor_pivots",
    )(meta, parts, across)


def finish_kernel(
    meta_ref,
    front_ref,
    child_ref,
    received_ref,
    beneath_ref,
    upper_parts_ref,
    wide_parts_ref,
    column_parts_ref,
    pivot_ref,
    out_ref,
    solved_ref,
    solved_parts_ref,
):
    half_step = pl.program_id(0)
    sibling = meta_ref[0]
    column_index = meta_ref[2]
    width = pivot_ref.shape[1]

    solve(
        lambda i: jnp.concatenate([beneath_ref[i, 0], beneath_ref[8 + i, 0]]),
        upper_parts_ref,
        wide_parts_ref,
        solved_ref,
        solved_parts_ref,
    )
    update = parts_dot(
        [ref[...] for ref in solved_parts_ref],
        [ref[...] for ref in column_parts_ref],
        ((1,), (1,)),
    )

    for half in range(2):
        group = 2 * half_step + half

        def row_slot(s, u):
            return meta_ref[4 + s * 8 + group * 2 + u]

        def column_slot(s, u):
            return meta_ref[20 + s * 2 + u]

        for m in range(3):
            for n in range(3):
                lanes = slice(n * TILE, (n + 1) * TILE)
                total = front_ref[m, half, :, lanes]
                for u in range(2):
                    for v in range(2):
                        if m - u in (0, 1) and n - v in (0, 1):
                            own = (row_slot(sibling, u) == m) & (column_slot(sibling, v) == n)
                            other = (row_slot(1 - sibling, u) == m) & (
                                column_slot(1 - sibling, v) == n
                            )
                            own_lanes = pl.ds(
                                pl.multiple_of((2 * v + sibling) * TILE, TILE), TILE
                            )
                            mine = child_ref[u, half, :, own_lanes]
                            theirs = received_ref[v, u, half]
                            total = total + jnp.where(own, mine, 0.0)
                            total = total + jnp.where(other, theirs, 0.0)
                top = half * width + m * TILE
                out_ref[m, half, :, lanes] = (
                    total - update[top : top + TILE, n * TILE : (n + 1) * TILE]
                )

    pivot_column = column_index < PIVOT_TILES
    own_column = pl.ds(pl.multiple_of(lax.rem(column_index, 8) * TILE, TILE), TILE)

    @pl.when(pivot_column)
    def _():
        for half in range(2):
            for m in range(3):
                top = half * width + m * TILE
                out_ref[m, half, :, :TILE] = solved_ref[top : top + TILE, own_column]

    @pl.when(half_step == 0)
    def _():
        out_ref[0, 0, :, :] = pivot_ref[...]


def finish(meta, front, child, received, beneath, upper, wide, column, pivot):
    width = front.shape[1]
    whole = pl.BlockSpec(memory_space=pltpu.VMEM)
    held = lambda *shape: [pltpu.VMEM(shape, jnp.bfloat16) for _ in range(PARTS)]
    out = pl.pallas_call(
        finish_kernel,
        grid=(2,),
        out_shape=jax.ShapeDtypeStruct((3, 4, TILE, width), jnp.float32),
        in_specs=[
            pl.BlockSpec(memory_space=pltpu.SMEM),
            pl.BlockSpec((3, 2, TILE, width), lambda g: (0, g, 0, 0)),
            pl.BlockSpec((2, 2, TILE, 4 * TILE), lambda g: (0, g, 0, 0)),
            pl.BlockSpec((2, 2, 2, TILE, TILE), lambda g: (0, 0, g, 0, 0)),
            pl.BlockSpec((16, 1, width, TILE), lambda g: (0, g, 0, 0)),
            [whole] * PARTS,
            [whole] * PARTS,
            [whole] * PARTS,
            whole,
        ],
        out_specs=pl.BlockSpec((3, 2, TILE, width), lambda g: (0, g, 0, 0)),
        scratch_shapes=[
            pltpu.VMEM((2 * width, NPIV), jnp.float32),
            held(2 * width, NPIV),
        ],
        compiler_params=pltpu.CompilerParams(vmem_limit_bytes=36 * 2**20),
        cost_estimate=pl.CostEstimate(
            flops=15 * 10**9, bytes_accessed=24 * 2**20, transcendentals=0
        ),
        name="solve_and_update",
    )(
        meta,
        front.reshape(3, 4, TILE, width),
        child.reshape(2, 4, TILE, 4 * TILE),
        received.reshape(2, 2, 4, TILE, TILE),
        beneath,
        upper,
        wide,
        column,
        pivot,
    )
    return out.reshape(front.shape)


ALL = ("pair", "row", "col")
SWAP = [(0, 1), (1, 0)]
RING = (0, 1, 7, 2, 6, 3, 5, 4)


def at(pair, row, col):
    return (pair * 8 + row) * 16 + col


def ring_gather(block, beside):
    up = [(i, (i + 1) % 8) for i in range(8)]
    down = [(i, (i - 1) % 8) for i in range(8)]
    half = block.shape[0] // 2
    behind = ahead = block
    blocks = [block]
    for turn in range(3):
        behind = lax.ppermute(behind, "row", up)
        ahead = lax.ppermute(ahead, "row", down)
        if turn:
            behind, ahead, beside[turn - 1] = lax.optimization_barrier(
                (behind, ahead, beside[turn - 1])
            )
        blocks += [behind, ahead]
    last = [lax.ppermute(behind[:half], "row", up), lax.ppermute(ahead[half:], "row", down)]
    return blocks + [jnp.concatenate(last)]


def assemble_kernel(meta_ref, front_ref, child_ref, came_ref, out_ref):
    sibling = meta_ref[0]
    own_row = meta_ref[4 + sibling * 8] == 0
    other_row = meta_ref[4 + (1 - sibling) * 8] == 0
    for n in range(3):
        total = front_ref[:, n * TILE : (n + 1) * TILE]
        for v in range(2):
            if n - v in (0, 1):
                own = own_row & (meta_ref[20 + sibling * 2 + v] == n)
                other = other_row & (meta_ref[20 + (1 - sibling) * 2 + v] == n)
                lanes = pl.ds(pl.multiple_of((2 * v + sibling) * TILE, TILE), TILE)
                total = total + jnp.where(own, child_ref[:, lanes], 0.0)
                total = total + jnp.where(other, came_ref[v], 0.0)
        out_ref[n * TILE : (n + 1) * TILE, :] = total.T


def assemble(meta, front, child, came):
    width = front.shape[1]
    return pl.pallas_call(
        assemble_kernel,
        grid=(1,),
        out_shape=jax.ShapeDtypeStruct((width, TILE), jnp.float32),
        in_specs=[
            pl.BlockSpec(memory_space=pltpu.SMEM),
            pl.BlockSpec((TILE, width), lambda g: (0, 0)),
            pl.BlockSpec((TILE, 4 * TILE), lambda g: (0, 0)),
            pl.BlockSpec((2, TILE, TILE), lambda g: (0, 0, 0)),
        ],
        out_specs=pl.BlockSpec((width, TILE), lambda g: (0, 0)),
        compiler_params=pltpu.CompilerParams(vmem_limit_bytes=8 * 2**20),
        name="assemble_pivot_rows",
    )(meta, front, child, came)


def body(front_init, child_blocks, tile_map):
    sibling = lax.axis_index("pair")
    row_index = lax.axis_index("row")
    col_index = lax.axis_index("col")
    half_index = col_index // 8
    column_index = sibling * 16 + col_index
    own = child_blocks[0]
    positions = tile_map.astype(jnp.int32).reshape(2, 2, 32) // 32

    def pick(count, v, even):
        low = own[:count, 2 * v * TILE : (2 * v + 1) * TILE]
        high = own[:count, (2 * v + 1) * TILE : 2 * (v + 1) * TILE]
        return jnp.where(even, low, high)

    with jax.named_scope("pivot_block"):
        own_positions = positions[sibling, 0]
        hit = (own_positions[row_index] == 0) & (own_positions[col_index] == 0)
        tile = jnp.where(sibling == 0, front_init[:TILE, :TILE], 0.0)
        tile = tile + jnp.where(hit, own[:TILE, :TILE], 0.0)
        upper_half, lower_half = tile[: TILE // 2], tile[TILE // 2 :]
        mine = jnp.where(half_index == 0, upper_half, 0.0)
        places = [(p, i, c) for p in range(2) for i in range(8) for c in range(8)]
        mine = (
            mine
            + lax.ppermute(upper_half, ALL, [(at(p, i, c), at(1 - p, i, c)) for p, i, c in places])
            + lax.ppermute(lower_half, ALL, [(at(p, i, c), at(p, i, c + 8)) for p, i, c in places])
            + lax.ppermute(
                lower_half, ALL, [(at(p, i, c), at(1 - p, i, c + 8)) for p, i, c in places]
            )
        )
    with jax.named_scope("siblings"):
        handed = jnp.stack([pick(NPIV, v, sibling != 0) for v in range(2)])
        handed, mine = lax.optimization_barrier((handed, mine))
        received = lax.ppermute(handed, "pair", SWAP)

    with jax.named_scope("pivot_gather"):
        mine = mine[None]
        for bit in (4, 2, 1):
            came = lax.ppermute(mine, "row", [(i, i ^ bit) for i in range(8)])
            mine = jnp.concatenate([mine, came])
        mine, received = lax.optimization_barrier((mine, received))
        parts = lax.all_gather(mine, "col")

    row_positions = jnp.swapaxes(
        lax.dynamic_index_in_dim(positions.reshape(2, 2, 4, 8), row_index, 3, keepdims=False), 1, 2
    )
    column_positions = lax.dynamic_index_in_dim(positions, column_index, 2, keepdims=False)
    meta = jnp.concatenate(
        [
            jnp.stack([sibling, row_index, column_index, column_index]),
            row_positions.reshape(16),
            column_positions.reshape(4),
        ]
    ).astype(jnp.int32)

    with jax.named_scope("pivot_rows"):
        pivot_columns = assemble(meta, front_init[:TILE], own[:TILE], received)

    with jax.named_scope("panel"):
        pivot_columns, mine = lax.optimization_barrier((pivot_columns, mine))
        routes = [[], []]
        for p in range(2):
            for i in range(8):
                for c in range(16):
                    half, other = divmod(c, 8)
                    for away in range(2):
                        target = at(p ^ away, other, 8 * half + i)
                        routes[away].append((at(p, i, c), target))
        beside = [lax.ppermute(pivot_columns, ALL, route) for route in routes]
        across = ring_gather(pivot_columns, beside)
        same, crossed = beside
        turned = jnp.where(
            sibling == 0, jnp.stack([same, crossed]), jnp.stack([crossed, same])
        )
        beneath = lax.all_gather(turned, "col")
        across, parts = lax.optimization_barrier((across, parts))

    with jax.named_scope("factor"):
        factors = factor(meta, parts, across)
    with jax.named_scope("finish"):
        return finish(meta, front_init, own, received, beneath, *factors)


def solution(mesh):
    return jax.shard_map(
        body,
        mesh=mesh,
        in_specs=(P("row", ("pair", "col")), P("pair", "row", "col"), P()),
        out_specs=P("row", ("pair", "col")),
        check_vma=False,
    )
```

```python
import jax
import jax.numpy as jnp
from jax import lax
from jax.experimental import pallas as pl
from jax.experimental.pallas import tpu as pltpu
from jax.sharding import PartitionSpec as P

TILE = 128
PIVOT_TILES = 8
NPIV = TILE * PIVOT_TILES
STRIP = 64
GROUP = 8
PARTS = 2
FACTOR_FLOPS = 50 * 10**9
EXACT = lax.Precision.HIGHEST


def exact_dot(a, b, contract=((1,), (0,))):
    return lax.dot_general(
        a, b, (contract, ((), ())), precision=EXACT, preferred_element_type=jnp.float32
    )


def split(x):
    parts = []
    for _ in range(PARTS):
        part = x.astype(jnp.bfloat16)
        x = x - part.astype(jnp.float32)
        parts.append(part)
    return parts


def parts_dot(a, b, contract):
    pairs = [(i, order - i) for order in range(len(a)) for i in range(order + 1)]
    return lax.dot_general(
        jnp.concatenate([a[i] for i, _ in pairs], axis=contract[0][0]),
        jnp.concatenate([b[j] for _, j in pairs], axis=contract[1][0]),
        (contract, ((), ())),
        preferred_element_type=jnp.float32,
    )


def factor_tile(block):
    row = lax.broadcasted_iota(jnp.int32, (TILE, TILE), 0)
    lane = lax.broadcasted_iota(jnp.int32, (TILE, TILE), 1)
    remaining = jnp.concatenate([block, (row == lane).astype(jnp.float32)], axis=1)
    group_row = lax.broadcasted_iota(jnp.int32, (GROUP, 2 * TILE), 0)

    def twice(x):
        return jnp.concatenate([x, x], axis=1)

    def tall(x, count):
        return jnp.concatenate([x] * (count // GROUP), axis=0)

    done = []
    for first in range(0, TILE, STRIP):
        strip = remaining[:STRIP]
        finished = []
        for k in range(0, STRIP, GROUP):
            at = first + k
            count = STRIP - k - GROUP
            top, beneath = strip[:GROUP], strip[GROUP:]
            columns, rows, corner, inverse = [], [], {}, []
            for t in range(GROUP):
                if count:
                    columns.append(jnp.broadcast_to(beneath[:, at + t : at + t + 1], (count, TILE)))
                rows.append(jnp.broadcast_to(top[t : t + 1], (GROUP, 2 * TILE)))
                for r in range(t + 1):
                    corner[r, t] = jnp.broadcast_to(
                        top[r : r + 1, at + t : at + t + 1], (GROUP, TILE)
                    )
            for r in range(GROUP):
                inverse.append(1.0 / corner[r, r])
                for t in range(r + 1, GROUP):
                    scale = corner[r, t] * inverse[r]
                    for u in range(t, GROUP):
                        product = corner[r, t] * corner[r, u]
                        corner[t, u] = corner[t, u] - product * inverse[r]
                    if count:
                        columns[t] = columns[t] - tall(scale, count) * columns[r]
                    rows[t] = rows[t] - twice(scale) * rows[r]
            if count:
                for t in range(GROUP):
                    share = columns[t] * tall(inverse[t], count)
                    beneath = beneath - twice(share) * tall(rows[t], count)
            result = None
            for t in range(GROUP):
                root = lax.rsqrt(corner[t, t])
                root = root * (1.5 - 0.5 * corner[t, t] * root * root)
                scaled = rows[t] * twice(root)
                result = scaled if t == 0 else jnp.where(group_row == t, scaled, result)
            finished.append(result)
            strip = beneath
        strip = jnp.concatenate(finished, axis=0)
        done.append(strip)
        if first + STRIP < TILE:
            change = exact_dot(strip[:, :TILE], strip, ((0,), (0,)))
            remaining = remaining[STRIP:] - change[first + STRIP :]
    whole = jnp.concatenate(done, axis=0)
    return jnp.where(lane >= row, whole[:, :TILE], 0.0), whole[:, TILE:]


def factor_kernel(row_ref, parts_ref, upper_ref, inverse_ref):
    for i in range(PIVOT_TILES):
        away = i ^ row_ref[0]
        place = (away & 1) * 4 + (away & 2) + (away >> 2)
        for c in range(i, PIVOT_TILES):
            for half in range(2):
                upper_ref[pl.ds(i * TILE + half * 64, 64), pl.ds(c * TILE, TILE)] = parts_ref[
                    half * 8 + c, place
                ]

    def step(j, carry):
        at = pl.ds(pl.multiple_of(j * TILE, TILE), TILE)
        upper, inverse = factor_tile(upper_ref[at, at])
        upper_ref[at, at] = upper
        inverse_ref[j] = inverse.T
        for now in range(PIVOT_TILES - 1):

            @pl.when(j == now)
            def _():
                here = slice(now * TILE, (now + 1) * TILE)
                after = slice((now + 1) * TILE, NPIV)
                solved = parts_dot(split(inverse), split(upper_ref[here, after]), ((1,), (0,)))
                upper_ref[here, after] = solved
                solved_parts = split(solved)
                for k in range(now + 1, PIVOT_TILES):
                    rows = slice(k * TILE, (k + 1) * TILE)
                    rest = slice(k * TILE, NPIV)
                    offset = (k - now - 1) * TILE
                    upper_ref[rows, rest] = upper_ref[rows, rest] - parts_dot(
                        [part[:, offset : offset + TILE] for part in solved_parts],
                        [part[:, offset:] for part in solved_parts],
                        ((0,), (0,)),
                    )

        return carry

    lax.fori_loop(0, PIVOT_TILES, step, 0)


def factor(row_index, parts):
    return pl.pallas_call(
        factor_kernel,
        out_shape=(
            jax.ShapeDtypeStruct((NPIV, NPIV), jnp.float32),
            jax.ShapeDtypeStruct((PIVOT_TILES, TILE, TILE), jnp.float32),
        ),
        in_specs=[
            pl.BlockSpec(memory_space=pltpu.SMEM),
            pl.BlockSpec(memory_space=pltpu.VMEM),
        ],
        out_specs=tuple(pl.BlockSpec(memory_space=pltpu.VMEM) for _ in range(2)),
        compiler_params=pltpu.CompilerParams(vmem_limit_bytes=24 * 2**20),
        cost_estimate=pl.CostEstimate(
            flops=FACTOR_FLOPS, bytes_accessed=9 * 2**20, transcendentals=0
        ),
        name="factor_pivots",
    )(row_index.astype(jnp.int32).reshape(1), parts)


def finish_kernel(
    meta_ref,
    front_ref,
    child_ref,
    received_ref,
    across_refs,
    beneath_ref,
    upper_ref,
    inverse_ref,
    out_ref,
    upper_parts_ref,
    wide_parts_ref,
    across_ref,
    solved_ref,
    solved_parts_ref,
):
    half_step = pl.program_id(0)
    sibling = meta_ref[0]
    row_index = meta_ref[1]
    column_index = meta_ref[2]
    width = across_ref.shape[1]
    column_rows = slice(2 * width, 3 * width)

    def solve(count, source):
        for j in range(PIVOT_TILES // 2):
            columns = slice(2 * j * TILE, 2 * (j + 1) * TILE)
            rest = jnp.concatenate([source(2 * j), source(2 * j + 1)], axis=1)
            if j:
                before = slice(0, 2 * j * TILE)
                rest = rest - parts_dot(
                    [ref[:count, before] for ref in solved_parts_ref],
                    [ref[before, columns] for ref in upper_parts_ref],
                    ((1,), (0,)),
                )
            result = parts_dot(split(rest), [ref[j] for ref in wide_parts_ref], ((1,), (0,)))
            solved_ref[:count, columns] = result
            for ref, part in zip(solved_parts_ref, split(result)):
                ref[:count, columns] = part

    def panel(i):
        return [beneath_ref[i, 0], beneath_ref[8 + i, 0]]

    @pl.when(half_step == 0)
    def _():
        for j in range(PIVOT_TILES // 2):
            rows = slice(2 * j * TILE, 2 * (j + 1) * TILE)
            after = slice(2 * (j + 1) * TILE, NPIV)
            if j < PIVOT_TILES // 2 - 1:
                for ref, part in zip(upper_parts_ref, split(upper_ref[rows, after])):
                    ref[rows, after] = part
            low, high = inverse_ref[2 * j], inverse_ref[2 * j + 1]
            between = upper_ref[
                2 * j * TILE : (2 * j + 1) * TILE, (2 * j + 1) * TILE : 2 * (j + 1) * TILE
            ]
            corner = -exact_dot(low, exact_dot(between, high))
            for ref, l, h, c in zip(wide_parts_ref, split(low), split(high), split(corner)):
                ref[j, :TILE, :TILE] = l
                ref[j, TILE:, TILE:] = h
                ref[j, :TILE, TILE:] = c
                ref[j, TILE:, :TILE] = jnp.zeros((TILE, TILE), jnp.bfloat16)

        for behind, ref in zip(RING, across_refs):
            across_ref[lax.rem(row_index - behind + 8, 8)] = ref[...]
        solve(3 * width, lambda i: jnp.concatenate(panel(i) + [across_ref[i]]))

    @pl.when(half_step > 0)
    def _():
        solve(2 * width, lambda i: jnp.concatenate(panel(i)))

    update = parts_dot(
        [ref[: 2 * width] for ref in solved_parts_ref],
        [ref[column_rows] for ref in solved_parts_ref],
        ((1,), (1,)),
    )

    for half in range(2):
        group = 2 * half_step + half

        def row_slot(s, u):
            return meta_ref[4 + s * 8 + group * 2 + u]

        def column_slot(s, u):
            return meta_ref[20 + s * 2 + u]

        for m in range(3):
            for n in range(3):
                lanes = slice(n * TILE, (n + 1) * TILE)
                total = front_ref[m, half, :, lanes]
                for u in range(2):
                    for v in range(2):
                        if m - u in (0, 1) and n - v in (0, 1):
                            own = (row_slot(sibling, u) == m) & (column_slot(sibling, v) == n)
                            other = (row_slot(1 - sibling, u) == m) & (
                                column_slot(1 - sibling, v) == n
                            )
                            own_lanes = pl.ds(
                                pl.multiple_of((2 * v + sibling) * TILE, TILE), TILE
                            )
                            mine = child_ref[u, half, :, own_lanes]
                            theirs = received_ref[v, u, half]
                            total = total + jnp.where(own, mine, 0.0)
                            total = total + jnp.where(other, theirs, 0.0)
                top = half * width + m * TILE
                out_ref[m, half, :, lanes] = (
                    total - update[top : top + TILE, n * TILE : (n + 1) * TILE]
                )

    pivot_column = column_index < PIVOT_TILES
    own_column = pl.ds(pl.multiple_of(lax.rem(column_index, 8) * TILE, TILE), TILE)

    @pl.when(pivot_column)
    def _():
        for half in range(2):
            for m in range(3):
                top = half * width + m * TILE
                out_ref[m, half, :, :TILE] = solved_ref[top : top + TILE, own_column]

    @pl.when(half_step == 0)
    def _():
        own_row = pl.ds(pl.multiple_of(row_index * TILE, TILE), TILE)
        for n in range(3):
            lanes = slice(n * TILE, (n + 1) * TILE)
            top = 2 * width + n * TILE
            out_ref[0, 0, :, lanes] = solved_ref[top : top + TILE, own_row].T

        @pl.when(pivot_column)
        def _():
            @pl.when(row_index < column_index)
            def _():
                out_ref[0, 0, :, :TILE] = upper_ref[own_row, own_column]

            @pl.when(row_index > column_index)
            def _():
                out_ref[0, 0, :, :TILE] = upper_ref[own_column, own_row].T

            @pl.when(row_index == column_index)
            def _():
                row = lax.broadcasted_iota(jnp.int32, (TILE, TILE), 0)
                lane = lax.broadcasted_iota(jnp.int32, (TILE, TILE), 1)
                tile = upper_ref[own_row, own_column]
                out_ref[0, 0, :, :TILE] = jnp.where(row > lane, tile.T, tile)


def finish(meta, front, child, received, across, beneath, upper, inverse):
    width = front.shape[1]
    whole = pl.BlockSpec(memory_space=pltpu.VMEM)
    held = lambda *shape: [pltpu.VMEM(shape, jnp.bfloat16) for _ in range(PARTS)]
    out = pl.pallas_call(
        finish_kernel,
        grid=(2,),
        out_shape=jax.ShapeDtypeStruct((3, 4, TILE, width), jnp.float32),
        in_specs=[
            pl.BlockSpec(memory_space=pltpu.SMEM),
            pl.BlockSpec((3, 2, TILE, width), lambda g: (0, g, 0, 0)),
            pl.BlockSpec((2, 2, TILE, 4 * TILE), lambda g: (0, g, 0, 0)),
            pl.BlockSpec((2, 2, 2, TILE, TILE), lambda g: (0, 0, g, 0, 0)),
            [whole] * 8,
            pl.BlockSpec((16, 1, width, TILE), lambda g: (0, g, 0, 0)),
            whole,
            whole,
        ],
        out_specs=pl.BlockSpec((3, 2, TILE, width), lambda g: (0, g, 0, 0)),
        scratch_shapes=[
            held(NPIV, NPIV),
            held(PIVOT_TILES // 2, 2 * TILE, 2 * TILE),
            pltpu.VMEM((8, width, TILE), jnp.float32),
            pltpu.VMEM((3 * width, NPIV), jnp.float32),
            held(3 * width, NPIV),
        ],
        compiler_params=pltpu.CompilerParams(vmem_limit_bytes=50 * 2**20),
        cost_estimate=pl.CostEstimate(
            flops=15 * 10**9, bytes_accessed=24 * 2**20, transcendentals=0
        ),
        name="solve_and_update",
    )(
        meta,
        front.reshape(3, 4, TILE, width),
        child.reshape(2, 4, TILE, 4 * TILE),
        received.reshape(2, 2, 4, TILE, TILE),
        across,
        beneath,
        upper,
        inverse,
    )
    return out.reshape(front.shape)


ALL = ("pair", "row", "col")
SWAP = [(0, 1), (1, 0)]
RING = (0, 1, 7, 2, 6, 3, 5, 4)


def at(pair, row, col):
    return (pair * 8 + row) * 16 + col


def ring_gather(block, beside):
    up = [(i, (i + 1) % 8) for i in range(8)]
    down = [(i, (i - 1) % 8) for i in range(8)]
    half = block.shape[0] // 2
    behind = ahead = block
    blocks = [block]
    for turn in range(3):
        behind = lax.ppermute(behind, "row", up)
        ahead = lax.ppermute(ahead, "row", down)
        if turn < len(beside):
            behind, ahead, beside[turn] = lax.optimization_barrier((behind, ahead, beside[turn]))
        blocks += [behind, ahead]
    last = [lax.ppermute(behind[:half], "row", up), lax.ppermute(ahead[half:], "row", down)]
    return blocks + [jnp.concatenate(last)]


def assemble_kernel(meta_ref, front_ref, child_ref, came_ref, out_ref):
    sibling = meta_ref[0]
    own_row = meta_ref[4 + sibling * 8] == 0
    other_row = meta_ref[4 + (1 - sibling) * 8] == 0
    for n in range(3):
        total = front_ref[:, n * TILE : (n + 1) * TILE]
        for v in range(2):
            if n - v in (0, 1):
                own = own_row & (meta_ref[20 + sibling * 2 + v] == n)
                other = other_row & (meta_ref[20 + (1 - sibling) * 2 + v] == n)
                lanes = pl.ds(pl.multiple_of((2 * v + sibling) * TILE, TILE), TILE)
                total = total + jnp.where(own, child_ref[:, lanes], 0.0)
                total = total + jnp.where(other, came_ref[v], 0.0)
        out_ref[n * TILE : (n + 1) * TILE, :] = total.T


def assemble(meta, front, child, came):
    width = front.shape[1]
    return pl.pallas_call(
        assemble_kernel,
        grid=(1,),
        out_shape=jax.ShapeDtypeStruct((width, TILE), jnp.float32),
        in_specs=[
            pl.BlockSpec(memory_space=pltpu.SMEM),
            pl.BlockSpec((TILE, width), lambda g: (0, 0)),
            pl.BlockSpec((TILE, 4 * TILE), lambda g: (0, 0)),
            pl.BlockSpec((2, TILE, TILE), lambda g: (0, 0, 0)),
        ],
        out_specs=pl.BlockSpec((width, TILE), lambda g: (0, 0)),
        compiler_params=pltpu.CompilerParams(vmem_limit_bytes=8 * 2**20),
        name="assemble_pivot_rows",
    )(meta, front, child, came)


def body(front_init, child_blocks, tile_map):
    sibling = lax.axis_index("pair")
    row_index = lax.axis_index("row")
    col_index = lax.axis_index("col")
    half_index = col_index // 8
    column_index = sibling * 16 + col_index
    own = child_blocks[0]
    positions = tile_map.astype(jnp.int32).reshape(2, 2, 32) // 32

    def pick(count, v, even):
        low = own[:count, 2 * v * TILE : (2 * v + 1) * TILE]
        high = own[:count, (2 * v + 1) * TILE : 2 * (v + 1) * TILE]
        return jnp.where(even, low, high)

    with jax.named_scope("pivot_block"):
        own_positions = positions[sibling, 0]
        hit = (own_positions[row_index] == 0) & (own_positions[col_index] == 0)
        tile = jnp.where(sibling == 0, front_init[:TILE, :TILE], 0.0)
        tile = tile + jnp.where(hit, own[:TILE, :TILE], 0.0)
        upper_half, lower_half = tile[: TILE // 2], tile[TILE // 2 :]
        mine = jnp.where(half_index == 0, upper_half, 0.0)
        places = [(p, i, c) for p in range(2) for i in range(8) for c in range(8)]
        mine = (
            mine
            + lax.ppermute(upper_half, ALL, [(at(p, i, c), at(1 - p, i, c)) for p, i, c in places])
            + lax.ppermute(lower_half, ALL, [(at(p, i, c), at(p, i, c + 8)) for p, i, c in places])
            + lax.ppermute(
                lower_half, ALL, [(at(p, i, c), at(1 - p, i, c + 8)) for p, i, c in places]
            )
        )
    with jax.named_scope("siblings"):
        handed = jnp.stack([pick(NPIV, v, sibling != 0) for v in range(2)])
        handed, mine = lax.optimization_barrier((handed, mine))
        received = lax.ppermute(handed, "pair", SWAP)

    with jax.named_scope("pivot_gather"):
        mine = mine[None]
        for bit in (4, 2, 1):
            came = lax.ppermute(mine, "row", [(i, i ^ bit) for i in range(8)])
            mine = jnp.concatenate([mine, came])
        mine, received = lax.optimization_barrier((mine, received))
        parts = lax.all_gather(mine, "col")

    row_positions = jnp.swapaxes(
        lax.dynamic_index_in_dim(positions.reshape(2, 2, 4, 8), row_index, 3, keepdims=False), 1, 2
    )
    column_positions = lax.dynamic_index_in_dim(positions, column_index, 2, keepdims=False)
    meta = jnp.concatenate(
        [
            jnp.stack([sibling, row_index, column_index, column_index]),
            row_positions.reshape(16),
            column_positions.reshape(4),
        ]
    ).astype(jnp.int32)

    with jax.named_scope("pivot_rows"):
        pivot_columns = assemble(meta, front_init[:TILE], own[:TILE], received)

    with jax.named_scope("panel"):
        pivot_columns, mine = lax.optimization_barrier((pivot_columns, mine))
        routes = [[], []]
        for p in range(2):
            for i in range(8):
                for c in range(16):
                    half, other = divmod(c, 8)
                    for away in range(2):
                        target = at(p ^ away, other, 8 * half + i)
                        routes[away].append((at(p, i, c), target))
        beside = [lax.ppermute(pivot_columns, ALL, route) for route in routes]
        across = ring_gather(pivot_columns, beside)
        same, crossed = beside
        turned = jnp.where(
            sibling == 0, jnp.stack([same, crossed]), jnp.stack([crossed, same])
        )
        beneath = lax.all_gather(turned, "col")
        across, parts = lax.optimization_barrier((across, parts))

    with jax.named_scope("factor"):
        upper, inverse = factor(row_index, parts)
    with jax.named_scope("finish"):
        return finish(meta, front_init, own, received, across, beneath, upper, inverse)


def solution(mesh):
    return jax.shard_map(
        body,
        mesh=mesh,
        in_specs=(P("row", ("pair", "col")), P("pair", "row", "col"), P()),
        out_specs=P("row", ("pair", "col")),
        check_vma=False,
    )
```
